32 devices in a mesh: seq: 4 (over z), row: 4 (over y, core), col: 2 (over x).
Axes of the slice: x: 2, y: 2, z: 4, core: 2. Of those that a mesh axis runs over, the one named last changes fastest.
Arguments:
- hidden_in: bfloat16 [16384, 768], P(('seq', 'row', 'col')), may hold values from -6 to 6
- w_query: float32 [768, 768], P('col', 'row'), may hold values from -0.21875 to 0.21875
- b_query: float32 [768], P('row'), may hold values from -3 to 3
- w_key: float32 [768, 768], P('col', 'row'), may hold values from -0.21875 to 0.21875
- w_value: float32 [768, 768], P('col', 'row'), may hold values from -0.21875 to 0.21875
- b_value: float32 [768], P('row'), may hold values from -3 to 3
- w_out: float32 [768, 768], P('row', 'col'), may hold values from -3.5 to 3.5
- b_out: float32 [768], P('col'), may hold values from -3 to 3
- gain_attn: float32 [768], P('col'), may hold values from 0.5 to 1.5
- bias_attn: float32 [768], P('col'), may hold values from -3 to 3
- w_in: float32 [768, 3072], P('col', 'row'), may hold values from -0.21875 to 0.21875
- b_in: float32 [3072], P('row'), may hold values from -3 to 3
- w_ffout: float32 [768, 3072], P('col', 'row'), may hold values from -0.109375 to 0.109375
- b_ffout: float32 [768], P('col'), may hold values from -3 to 3
- gain_ffn: float32 [768], P('col'), may hold values from 0.5 to 1.5
- bias_ffn: float32 [768], P('col'), may hold values from -3 to 3
- glob_pos: int32 [4, 16], P('seq'), may hold values from 0 to 2047, as said below
- cotangent: bfloat16 [16384, 768], P(('seq', 'row', 'col')), may hold values from -6 to 6
Outputs:
- hidden_out: float32 [16384, 768], P(('seq', 'row', 'col'))
- grad_x: float32 [16384, 768], P(('seq', 'row', 'col'))
- grad_w_query: float32 [768, 768], P('col', 'row')
- grad_b_query: float32 [768], P('row')
- grad_w_key: float32 [768, 768], P('col', 'row')
- grad_w_value: float32 [768, 768], P('col', 'row')
- grad_b_value: float32 [768], P('row')
- grad_w_out: float32 [768, 768], P('row', 'col')
- grad_b_out: float32 [768], P('col')
- grad_gain_attn: float32 [768], P('col')
- grad_bias_attn: float32 [768], P('col')
- grad_w_in: float32 [768, 3072], P('col', 'row')
- grad_b_in: float32 [3072], P('row')
- grad_w_ffout: float32 [768, 3072], P('col', 'row')
- grad_b_ffout: float32 [768], P('col')
- grad_gain_ffn: float32 [768], P('col')
- grad_bias_ffn: float32 [768], P('col')
The draws below stay inside these ranges and needn't reach their ends.
Inputs may be any that keep to these rules, and one draw needn't show every extreme that they name: `glob_pos`: the 16 positions listed for one prompt are distinct, and position 0 is one of them.
All inputs are finite; a program needn't handle non-finite values.
Results may differ from the reference program's by a relative error of at most 0.017.
The reference program's roundings to bfloat16 on the way count: a program that leaves them out, or rounds other values in their place, can miss the bound.
Values may be sent and summed in bfloat16 or wider, within the bound.
No kernel may reach another device: no remote copies, remote signals or barrier semaphores. Data moves between devices by JAX's collectives and lax.ppermute only.
A program may use at most 320 MiB of HBM per device.

```python
import jax
import jax.numpy as jnp
from jax import lax

D = 768
HEADS = 12
HDIM = 64
FF = 3072
WIN = 256
PLEN = 2048
LC = 256
NG = 16
TS = 4096
TOKENS = 16384
N_SEQ = 4


def draw_glob_pos(key, part):
    subkeys = jax.random.split(key, N_SEQ)

    def one_prompt(subkey):
        order = jax.random.permutation(subkey, PLEN - 1) + 1
        return jnp.concatenate([jnp.zeros((1,), jnp.int32), order[:NG - 1].astype(jnp.int32)])
    return jax.vmap(one_prompt)(subkeys).reshape(N_SEQ, NG)


def level_of(own_key, shape, pieces, smallest, largest):
    level, own = 1.0, jax.random.fold_in(own_key, 6)
    for axis_at, parts in pieces:
        draws = jnp.exp(jax.random.uniform(jax.random.fold_in(own, axis_at), (parts,), jnp.float32, smallest / len(pieces), largest / len(pieces)))
        level = level * jnp.repeat(draws, shape[axis_at] // parts).reshape([-1 if axis == axis_at else 1 for axis in range(len(shape))])
    return level


def centred(own_key, extent, width, bound, pieces=(), kind=jnp.bfloat16):
    values = width * jax.random.normal(own_key, extent, jnp.float32)
    if pieces:
        values = values * level_of(own_key, extent, pieces, -0.22, 0.18)
    return jnp.clip(values, -bound, bound).astype(kind)


def setup_inputs(seed: int = 0) -> dict:
    key_list = jax.random.split(jax.random.key(seed), 19)
    hidden_in = centred(key_list[0], (TOKENS, D), 1.0, 6.0, ((0, 32),))
    w_query = centred(key_list[1], (D, D), D ** -0.5, 0.21875, ((0, 2), (1, 4)), jnp.float32)
    b_query = centred(key_list[2], (D,), 0.5, 3.0, ((0, 4),), jnp.float32)
    w_key = centred(key_list[3], (D, D), D ** -0.5, 0.21875, ((0, 2), (1, 4)), jnp.float32)
    w_value = centred(key_list[4], (D, D), D ** -0.5, 0.21875, ((0, 2), (1, 4)), jnp.float32)
    b_value = centred(key_list[5], (D,), 0.5, 3.0, ((0, 4),), jnp.float32)
    w_out = centred(key_list[6], (D, D), (max(1, D // 256)) ** -0.5, 3.5, ((0, 4), (1, 2)), jnp.float32)
    b_out = centred(key_list[7], (D,), 0.5, 3.0, ((0, 2),), jnp.float32)
    gain_attn = jnp.clip(1.0 + 0.1 * jax.random.normal(key_list[8], (D,), jnp.float32), 0.5, 1.5)
    bias_attn = centred(key_list[9], (D,), 0.5, 3.0, ((0, 2),), jnp.float32)
    w_in = centred(key_list[10], (D, FF), D ** -0.5, 0.21875, ((0, 2), (1, 4)), jnp.float32)
    b_in = centred(key_list[11], (FF,), 0.5, 3.0, ((0, 4),), jnp.float32)
    w_ffout = centred(key_list[12], (D, FF), FF ** -0.5, 0.109375, ((0, 2), (1, 4)), jnp.float32)
    b_ffout = centred(key_list[13], (D,), 0.5, 3.0, ((0, 2),), jnp.float32)
    gain_ffn = jnp.clip(1.0 + 0.1 * jax.random.normal(key_list[14], (D,), jnp.float32), 0.5, 1.5)
    bias_ffn = centred(key_list[15], (D,), 0.5, 3.0, ((0, 2),), jnp.float32)
    glob_pos = draw_glob_pos(jax.random.fold_in(key_list[18], 71), 0)
    cotangent = centred(key_list[17], (TOKENS, D), 1.0, 6.0, ((0, 32),))
    return {"hidden_in": hidden_in, "w_query": w_query, "b_query": b_query, "w_key": w_key, "w_value": w_value, "b_value": b_value, "w_out": w_out, "b_out": b_out, "gain_attn": gain_attn, "bias_attn": bias_attn, "w_in": w_in, "b_in": b_in, "w_ffout": w_ffout, "b_ffout": b_ffout, "gain_ffn": gain_ffn, "bias_ffn": bias_ffn, "glob_pos": glob_pos, "cotangent": cotangent}


@jax.custom_vjp
def low(v):
    return lax.optimization_barrier(v.astype(jnp.bfloat16)).astype(jnp.float32)

@jax.custom_vjp
def low_back(v):
    return v

def low_keep(v):
    return (low(v), None)

def low_pass(kept, grad):
    return (grad,)

def back_keep(v):
    return (v, None)

def back_low(kept, grad):
    return (low(grad),)
low.defvjp(low_keep, low_pass)
low_back.defvjp(back_keep, back_low)

def matmul(left, right):
    return jnp.dot(left, right, precision=lax.Precision.HIGHEST)

def token_meta(index, glob_row):
    is_prompt = index < PLEN
    after = jnp.maximum(index - PLEN, 0)
    member = after // LC
    within = after % LC
    place = jnp.where(is_prompt, index, PLEN + within)
    listed = glob_row[None, :] == place[:, None]
    is_global = is_prompt & jnp.any(listed, axis=1)
    return (is_prompt, place, member, is_global)

def visible(query_meta, key_meta):
    query_prompt, query_place, query_member, query_global = query_meta
    key_prompt, key_place, key_member, key_global = key_meta
    nearby = jnp.abs(query_place[:, None] - key_place[None, :]) <= WIN
    reach = nearby | key_global[None, :] | (query_global & query_prompt)[:, None]
    shared = key_prompt[None, :] & reach
    own_cont = (~key_prompt)[None, :] & (~query_prompt)[:, None] & (query_member[:, None] == key_member[None, :])
    return shared | own_cont

def attend_block(query_block, seq_id, first_row, key_all, value_all, glob_pos):
    key_seq = lax.dynamic_index_in_dim(key_all, seq_id, 0, keepdims=False)
    value_seq = lax.dynamic_index_in_dim(value_all, seq_id, 0, keepdims=False)
    glob_row = lax.dynamic_index_in_dim(glob_pos, seq_id, 0, keepdims=False)
    key_index = jnp.arange(TS, dtype=jnp.int32)
    query_index = first_row + jnp.arange(LC, dtype=jnp.int32)
    allow = visible(token_meta(query_index, glob_row), token_meta(key_index, glob_row))
    scores = jnp.einsum('qhd,khd->hqk', query_block, key_seq, precision=lax.Precision.HIGHEST) * 0.125
    scores = low_back(scores)
    scores = jnp.where(allow[None], scores, -1e+30)
    peak = lax.optimization_barrier(jnp.max(scores, axis=-1, keepdims=True))
    raised = jnp.exp(scores - peak)
    shares = low(raised / lax.optimization_barrier(jnp.sum(raised, axis=-1, keepdims=True)))
    return jnp.einsum('hqk,khd->qhd', shares, value_seq, precision=lax.Precision.HIGHEST)

def layer_norm(resid, gain, shift):
    center = lax.optimization_barrier(jnp.mean(resid, axis=-1, keepdims=True))
    spread = lax.optimization_barrier(jnp.mean(jnp.square(resid - center), axis=-1, keepdims=True))
    return (resid - center) * lax.rsqrt(spread + 1e-05) * gain + shift

def layer(hidden_in, w_query, b_query, w_key, w_value, b_value, w_out, b_out, gain_attn, bias_attn, w_in, b_in, w_ffout, b_ffout, gain_ffn, bias_ffn, glob_pos):
    query = low(low_back(matmul(hidden_in, low(w_query)) + b_query))
    keyed = low(low_back(matmul(hidden_in, low(w_key))))
    valued = low(low_back(matmul(hidden_in, low(w_value)) + b_value))
    blocks_total = N_SEQ * TS // LC
    per_seq = TS // LC
    order = jnp.arange(blocks_total, dtype=jnp.int32)
    seq_ids = order // per_seq
    first_rows = order % per_seq * LC
    key_all = keyed.reshape(N_SEQ, TS, HEADS, HDIM)
    value_all = valued.reshape(N_SEQ, TS, HEADS, HDIM)
    query_blocks = query.reshape(blocks_total, LC, HEADS, HDIM)
    attend = jax.checkpoint(attend_block)
    mixed = lax.map(lambda item: attend(item[0], item[1], item[2], key_all, value_all, glob_pos), (query_blocks, seq_ids, first_rows))
    mixed = low(low_back(mixed.reshape(N_SEQ * TS, D)))
    branch = low_back(matmul(mixed, low(w_out)) + b_out)
    hidden = layer_norm(hidden_in + branch, gain_attn, bias_attn)
    inner = low_back(matmul(low(hidden), low(w_in)) + b_in)
    active = low(jax.nn.gelu(inner, approximate=False))
    update = low_back(matmul(active, low(w_ffout).T) + b_ffout)
    return layer_norm(hidden + update, gain_ffn, bias_ffn)

def reference(hidden_in, w_query, b_query, w_key, w_value, b_value, w_out, b_out, gain_attn, bias_attn, w_in, b_in, w_ffout, b_ffout, gain_ffn, bias_ffn, glob_pos, cotangent):
    floats = (hidden_in, w_query, b_query, w_key, w_value, b_value, w_out, b_out, gain_attn, bias_attn, w_in, b_in, w_ffout, b_ffout, gain_ffn, bias_ffn)
    floats = tuple((item.astype(jnp.float32) for item in floats))

    def forward(*arrays):
        return layer(*arrays, glob_pos)
    result, pullback = jax.vjp(forward, *floats)
    grads = pullback(cotangent.astype(jnp.float32))
    return (result, grads[0], grads[1], grads[2], grads[3], grads[4], grads[5], grads[6], grads[7], grads[8], grads[9], grads[10], grads[11], grads[12], grads[13], grads[14], grads[15])
```

```python
import functools

import jax
import jax.numpy as jnp
from jax import lax
from jax.experimental import pallas as pl
from jax.experimental.pallas import tpu as pltpu
from jax.sharding import PartitionSpec as P

D = 768
HDIM = 64
WIN = 256
PLEN = 2048
LC = 256
PAIR = 2 * HDIM
FAR = -(1 << 20)
BF = jnp.bfloat16
F32 = jnp.float32
NEG = -1e30

NN = (((1,), (0,)), ((), ()))
NT = (((1,), (1,)), ((), ()))
TN = (((0,), (0,)), ((), ()))


def dot(a, b, dims=NN):
    return lax.dot_general(a, b, dims, preferred_element_type=F32)


def swap(value, step):
    axis, bit = step
    size = lax.axis_size(axis)
    return lax.ppermute(value, axis, [(i, i ^ bit) for i in range(size)])


def far_steps():
    rows, cols = lax.axis_size("row"), lax.axis_size("col")
    steps, bit = [], 1
    while bit < cols:
        steps.append(("col", bit))
        bit *= 2
    bit = 2
    while bit < rows:
        steps.append(("row", bit))
        bit *= 2
    return steps


NEAR = ("row", 1)


def move(name, step):
    axis, bit = step
    return (name[0] ^ bit, name[1]) if axis == "row" else (name[0], name[1] ^ bit)


def fence(*values):
    return lax.optimization_barrier(values)


def swap_both(value, row_bit, col_bit):
    rows, cols = lax.axis_size("row"), lax.axis_size("col")
    pairs = [
        (r * cols + c, (r ^ row_bit) * cols + (c ^ col_bit))
        for r in range(rows)
        for c in range(cols)
    ]
    return lax.ppermute(value, ("row", "col"), pairs)


def far_names():
    rows, cols = lax.axis_size("row"), lax.axis_size("col")
    return [(a, b) for a in range(0, rows, 2) for b in range(cols) if (a, b) != (0, 0)]


def gather_far(own):
    return {(0, 0): own} | {name: swap_both(own, *name) for name in far_names()}


def gather_near(pieces):
    return pieces | {move(k, NEAR): swap(v, NEAR) for k, v in pieces.items()}


def in_order(parts, me):
    bit = 1
    while bit < len(parts):
        odd = (me & bit) != 0
        parts = [jnp.where(odd, parts[t ^ bit], parts[t]) for t in range(len(parts))]
        bit *= 2
    return parts


def near_kernel(at_ref, keep_ref, got_ref, *out_refs, col_n):
    for half in range(keep_ref.shape[0]):
        near = keep_ref[half].astype(F32) + got_ref[half].astype(F32)
        for b, part in enumerate(columns(near, col_n, at_ref[1])):
            out = out_refs[half * col_n + b]
            out[...] = part.astype(out.dtype)


def near_pieces(at, keep, got, col_n):
    halves, length, width = keep.shape
    count = halves * col_n
    piece = (length, width // col_n)
    shapes = [jax.ShapeDtypeStruct(piece, BF if i else F32) for i in range(count)]
    return pl.pallas_call(
        functools.partial(near_kernel, col_n=col_n),
        in_specs=[SCALAR] + [pl.BlockSpec(memory_space=pltpu.VMEM)] * 2,
        out_shape=to_hbm(shapes),
        compiler_params=params(24),
        name="near_pieces",
    )(*hbm(at, keep, got))


def far_sum(parts):
    cols = lax.axis_size("col")
    total = parts[0]
    for a, b in far_names():
        total = total + swap_both(parts[a // 2 * cols + b], a, b).astype(F32)
    return total


def seq_sum(value):
    count, me = lax.axis_size("seq"), lax.axis_index("seq")
    parts = value.astype(BF).reshape((count, value.shape[0] // count) + value.shape[1:])

    def turn(part, k):
        return lax.ppermute(part, "seq", [(i, (i + k) % count) for i in range(count)])

    total = lax.dynamic_index_in_dim(parts, me, 0, keepdims=False).astype(F32)
    for k in range(1, count):
        part = lax.dynamic_index_in_dim(parts, (me + k) % count, 0, keepdims=False)
        total = total + turn(part, k).astype(F32)
    own = total.astype(BF)
    held = jnp.stack([own] + [turn(own, k) for k in range(1, count)])
    out = [lax.dynamic_index_in_dim(held, (me - i) % count, 0, keepdims=False) for i in range(count)]
    return jnp.concatenate(out, axis=0).astype(F32)


def group_sum(value, merge):
    for step in far_steps() + [NEAR]:
        value = merge(value, swap(value, step), step)
    return value


def shift(value, pairs):
    return lax.ppermute(value, ("row", "col"), pairs) if pairs else jnp.zeros_like(value)


class Halo:
    def __init__(self, rows, devices):
        self.rows = rows
        self.n = devices
        self.half = PLEN // rows
        self.block = min(rows, WIN)
        self.steps = WIN // self.block
        self.wide = rows >= 2 * WIN

    def pairs_left(self, t):
        return [(j - t, j) for j in range(self.half) if j >= t]

    def pairs_right(self, t):
        return [(j + t, j) for j in range(self.half) if j + t < self.half]

    def pairs_mates(self, t):
        return [(self.mate(j, t), j) for j in range(self.half, self.n)]

    def mate(self, j, t):
        base = j - j % self.steps
        return base + (j - base + t) % self.steps

    def tree(self, t):
        source = self.half - self.steps + t
        rounds, bit = [[(source, source + self.half)]], 1
        have = [source + self.half]
        while len(have) < self.n - self.half:
            rounds.append([(d, d ^ bit) for d in have])
            have += [d ^ bit for d in have]
            bit *= 2
        return rounds

    def fetch(self, own, is_prompt):
        first, last = own[: self.block], own[-self.block :]
        left, right, tail = [], [], []
        for t in range(self.steps, 0, -1):
            at = self.steps - t
            rounds = self.tree(at)
            if self.steps == 1:
                left.append(shift(last, self.pairs_left(t) + rounds[0]))
                mixed = jnp.where(is_prompt, first, left[0])
                right.append(shift(mixed, self.pairs_right(t) + rounds[1]))
                held = left[0] + jnp.where(is_prompt, jnp.zeros((), BF), right[0])
                rounds = rounds[2:]
            else:
                left.append(shift(last, self.pairs_left(t)))
                right.append(shift(first, self.pairs_right(at + 1)))
                held = shift(last, rounds[0])
                rounds = rounds[1:]
            for pairs in rounds:
                held = held + shift(held, pairs)
            tail.append(held)
        hop = left[0]
        left = [jnp.where(is_prompt, a, b) for a, b in zip(left, tail)]
        if self.wide:
            right = [jnp.where(is_prompt, a, b) for a, b in zip(right, tail)]
        elif self.steps > 1:
            mates = [shift(own, self.pairs_mates(t)) for t in range(1, self.steps)]
            right = [jnp.where(is_prompt, a, b) for a, b in zip(right, mates)] + right[len(mates) :]
        return jnp.concatenate(left, axis=0), jnp.concatenate(right, axis=0), hop

    def give(self, left, right, is_prompt):
        block = self.block

        def cut(value):
            return [value[t * block : (t + 1) * block] for t in range(self.steps)]

        def back(value, pairs):
            return shift(value, [(b, a) for a, b in pairs]).astype(F32)

        zero = jnp.zeros((), F32)
        left, right = cut(left), cut(right)
        first = jnp.zeros((block, left[0].shape[1]), F32)
        last = first
        for i, t in enumerate(range(self.steps, 0, -1)):
            last = last + back(left[i].astype(BF), self.pairs_left(t))
        for i, t in enumerate(range(1, self.steps + 1)):
            first = first + back(right[i].astype(BF), self.pairs_right(t))
        for t in range(self.steps):
            held = left[t] + right[t] if self.wide else left[t]
            held = jnp.where(is_prompt, zero, held)
            rounds = self.tree(t)
            for pairs in reversed(rounds[1:]):
                held = held + back(held.astype(BF), pairs)
            last = last + back(held.astype(BF), rounds[0])
        if not self.wide:
            for t in range(1, self.steps):
                first = first + back(right[t - 1].astype(BF), self.pairs_mates(t))
        return first, last

    def key_rows(self, me, is_prompt):
        near = jnp.arange(WIN, dtype=jnp.int32)
        start = me * self.rows
        left = start - WIN + near
        left = jnp.where(left < 0, FAR, left)
        left = jnp.where(is_prompt, left, PLEN - WIN + near)
        right = start + self.rows + near
        right = jnp.where(right < PLEN, right, FAR)
        if self.wide:
            other = PLEN - WIN + near
        elif self.steps > 1:
            parts = [
                (me - me % self.steps + (me % self.steps + t) % self.steps) * self.rows
                + jnp.arange(self.rows, dtype=jnp.int32)
                for t in range(1, self.steps)
            ]
            other = jnp.concatenate(parts + [jnp.full((self.rows,), FAR, jnp.int32)])
        else:
            other = jnp.full((WIN,), FAR, jnp.int32)
        right = jnp.where(is_prompt, right, other)
        own = start + jnp.arange(self.rows, dtype=jnp.int32)
        return jnp.concatenate([left, own, right])


def place_of(index):
    after = index - PLEN
    return jnp.where(index < PLEN, index, PLEN + after % LC)


def bias_blocks(query_rows, key_rows, glob_row, block):
    count = query_rows.shape[0] // block
    query = query_rows.reshape(count, block, 1)
    keys = jnp.stack([key_rows[i * block : i * block + 2 * WIN + block] for i in range(count)])
    keys = keys[:, None, :]
    near = (jnp.abs(place_of(query) - keys) <= WIN) & (keys < PLEN) & (keys >= 0)
    same = (query >= PLEN) & (keys >= PLEN) & ((query - PLEN) // LC == (keys - PLEN) // LC)
    window = jnp.where(near | same, 0.0, NEG).astype(F32)
    beyond = jnp.abs(place_of(query) - glob_row[None, None, :]) > WIN
    return window, jnp.where(beyond, 0.0, NEG).astype(F32)


def lanes(shape):
    return lax.broadcasted_iota(jnp.int32, shape, 1) < HDIM


def one_head(value, half, scale):
    keep = lanes(value.shape)
    keep = keep if half == 0 else ~keep
    return (jnp.where(keep, value.astype(F32), 0.0) * scale).astype(BF)


def stacked(value, scale):
    head = lax.broadcasted_iota(jnp.int32, value.shape, 1) // HDIM
    value = value.astype(F32) * scale
    parts = [jnp.where(head == h, value, 0.0) for h in range(value.shape[1] // HDIM)]
    return jnp.concatenate(parts, axis=0)


def unstacked(value, count):
    shape = (count, value.shape[1])
    head = lax.broadcasted_iota(jnp.int32, shape, 1) // HDIM
    out = jnp.zeros(shape, F32)
    for h in range(value.shape[0] // count):
        out = jnp.where(head == h, value[h * count : (h + 1) * count, :], out)
    return out


def glob_state(q, k, v, keep):
    count, wide = q.shape
    s = dot(stacked(q, 0.125).astype(BF), k, NT) + keep
    m = jnp.max(s, axis=1, keepdims=True)
    p = jnp.exp(s - m)
    total = jnp.sum(p, axis=1, keepdims=True)
    o = dot(p.astype(BF), v)
    return [unstacked(jnp.broadcast_to(t, o.shape), count) for t in (o, m, total)]


def share_rows(refs, share, kind):
    at = (share * 3 + kind) * HDIM
    return jnp.concatenate([r[at : at + HDIM, :] for r in refs], axis=0)


def columns(value, count, me):
    size = value.shape[1] // count
    return in_order([value[:, c * size : (c + 1) * size] for c in range(count)], me)


def project_kernel(at_ref, keep_ref, bq_ref, bv_ref, *refs, row_n, col_n):
    xs, pieces = refs[:4], refs[4 : 4 + row_n * col_n]
    q_ref, qg_ref, k_ref, v_ref, state_ref = refs[4 + row_n * col_n :]
    col = at_ref[1]
    span = row_n * HDIM
    mats = []
    for b in range(col_n):
        refs_b = [pieces[a * col_n + b] for a in range(row_n)]
        mats.append(jnp.concatenate([share_rows(refs_b, 0, kind) for kind in range(3)], axis=0))

    at = 0
    for g, x in enumerate(xs):
        rows = slice(at, at + x.shape[0])
        at += x.shape[0]
        first = 0 if g in (1, 3) else span
        total = 0.0
        for part, mat in zip(columns(x[...], col_n, col), mats):
            total = total + dot(part, mat[first:, :], NT)
        k_ref[rows, :] = total[:, span - first : 2 * span - first].astype(BF)
        v_ref[rows, :] = (total[:, 2 * span - first :] + bv_ref[...]).astype(BF)
        if first == 0:
            out = q_ref if g == 1 else qg_ref
            out[...] = (total[:, :span] + bq_ref[...]).astype(BF)
    rows = slice(xs[0].shape[0], xs[0].shape[0] + xs[1].shape[0])
    state = glob_state(qg_ref[...], k_ref[rows, :], v_ref[rows, :], keep_ref[...])
    for i in range(3):
        state_ref[i] = state[i]


def swap_heads(value, bit):
    blocks = [value[..., i * PAIR : (i + 1) * PAIR] for i in range(value.shape[-1] // PAIR)]
    if bit == 1:
        return [pltpu.roll(v, HDIM, v.ndim - 1) for v in blocks]
    return [blocks[i ^ (bit // 2)] for i in range(len(blocks))]


def merge_kernel(one_ref, two_ref, out_ref, *, bit):
    for i in range(one_ref.shape[2] // PAIR):
        span = slice(i * PAIR, (i + 1) * PAIR)
        o1, m1, l1 = [one_ref[j, :, span] for j in range(3)]
        o2, m2, l2 = [swap_heads(two_ref[j], bit)[i] for j in range(3)]
        top = jnp.maximum(m1, m2)
        a, b = jnp.exp(m1 - top), jnp.exp(m2 - top)
        out_ref[0, :, span] = o1 * a + o2 * b
        out_ref[1, :, span] = top
        out_ref[2, :, span] = l1 * a + l2 * b


def add_heads_kernel(one_ref, two_ref, out_ref, *, bit):
    for i, block in enumerate(swap_heads(two_ref[...].astype(F32), bit)):
        span = slice(i * PAIR, (i + 1) * PAIR)
        out_ref[:, span] = (one_ref[:, span].astype(F32) + block).astype(BF)


def head_bit(step):
    return step[1] if step[0] == "row" else 0


def merge_states(one, two, step):
    return pl.pallas_call(
        functools.partial(merge_kernel, bit=head_bit(step)),
        out_shape=jax.ShapeDtypeStruct(one.shape, one.dtype),
        name="merge_states",
    )(one, two)


def add_heads(one, two, step):
    return pl.pallas_call(
        functools.partial(add_heads_kernel, bit=head_bit(step)),
        out_shape=jax.ShapeDtypeStruct(one.shape, one.dtype),
        name="add_heads",
    )(one, two)


def chunks(rows):
    size = min(rows, 128)
    return [slice(i, i + size) for i in range(0, rows, size)]


def gelu_parts(u):
    density = jnp.exp(u * u * -0.5)
    t = 1.0 / (1.0 + 0.2316418863 * jnp.abs(u))
    poly = 1.061405429 * t - 1.453152027
    poly = poly * t + 1.421413741
    poly = poly * t - 0.284496736
    poly = poly * t + 0.254829592
    tail = 0.5 * poly * t * density
    phi = jnp.where(u >= 0.0, 1.0 - tail, tail)
    return u * phi, phi + u * density * 0.3989422804014327


def column_sum(value):
    return jnp.sum(value, axis=0, keepdims=True)


def mlp_forward_kernel(*refs, row_n, col_n, calls):
    o_parts = refs[:calls]
    (
        at_ref, state_ref, pick_ref, x_ref, wraw_ref, vec_ref, bin_ref, win_ref, wff_ref, cot_ref,
        out_ref, low_ref, normed_ref, scale_ref, slope_ref, dres_ref, df_ref, gff_ref, sums_ref,
        o_ref, og_ref, lse_ref, wo_ref, act_ref, f_ref, hid_ref, dft_ref, u_ref,
    ) = refs[calls:]
    step = pl.program_id(0)
    rows, width = x_ref.shape
    deep, local = width // col_n, width // (row_n * HDIM)

    @pl.when(step == 0)
    def _():
        for a in range(row_n):
            for c in range(col_n):
                raw = wraw_ref[jnp.bitwise_xor(at_ref[0], a) * col_n + c]
                for i in range(local):
                    at = (i * row_n + a) * HDIM
                    wo_ref[at : at + HDIM, c * deep : (c + 1) * deep] = raw[
                        i * HDIM : (i + 1) * HDIM, :
                    ]
        og = state_ref[0] / state_ref[2]
        og_ref[...] = og
        lse_ref[...] = state_ref[1] + jnp.log(state_ref[2])
        og = og.astype(BF)
        for cut in chunks(rows):
            pick = pick_ref[cut, :]
            is_glob = jnp.sum(pick.astype(F32), axis=1, keepdims=True) > 0.5
            o = jnp.concatenate([r[cut, :] for r in o_parts], axis=1)
            o_ref[cut, :] = jnp.where(is_glob, dot(pick, og), o.astype(F32)).astype(BF)
        f_ref[...] = dot(o_ref[...], wo_ref[...])
        for cut in chunks(rows):
            resid = x_ref[cut, :].astype(F32) + f_ref[cut, :] + vec_ref[0:1, :]
            hidden, normed, scale = norm_forward(resid, vec_ref[1:2, :], vec_ref[2:3, :])
            hid_ref[cut, :] = hidden
            low_ref[cut, :] = hidden.astype(BF)
            normed_ref[cut, :] = normed
            scale_ref[cut, :] = jnp.broadcast_to(scale, (scale.shape[0], scale_ref.shape[1]))
        f_ref[...] = jnp.zeros_like(f_ref)

    @pl.when(step < row_n)
    def _():
        u_ref[...] = dot(low_ref[...], win_ref[...].reshape(width, -1))
        for cut in chunks(rows):
            act, slope = gelu_parts(u_ref[cut, :] + bin_ref[step])
            act_ref[step, cut, :] = act.astype(BF)
            slope_ref[0, cut, :] = slope
        f_ref[...] += dot(act_ref[step], wff_ref[...].reshape(width, -1), NT)

    @pl.when(step == row_n - 1)
    def _():
        gain, bias, low = 0.0, 0.0, 0.0
        for cut in chunks(rows):
            resid = hid_ref[cut, :] + f_ref[cut, :] + vec_ref[3:4, :]
            out, normed, scale = norm_forward(resid, vec_ref[4:5, :], vec_ref[5:6, :])
            out_ref[cut, :] = out
            g = cot_ref[cut, :].astype(F32)
            d = norm_backward(g, normed, scale, vec_ref[4:5, :])
            dres_ref[cut, :] = d
            d_low = d.astype(BF)
            df_ref[cut, :] = d_low
            dft_ref[:, cut] = d_low.T
            gain = gain + column_sum(g * normed)
            bias = bias + column_sum(g)
            low = low + column_sum(d_low.astype(F32))
        sums_ref[0:1, :] = gain
        sums_ref[1:2, :] = bias
        sums_ref[2:3, :] = low
        sums_ref[3:8, :] = jnp.zeros((5, sums_ref.shape[1]), F32)

    @pl.when(step >= row_n)
    def _():
        grad = dot(dft_ref[...], act_ref[step - row_n]).astype(BF)
        gff_ref[0, :, 0] = grad.reshape(col_n, deep, -1)


def mlp_backward_kernel(
    df_ref, slope_ref, win_ref, wff_ref, low_ref, dres_ref, normed_ref, scale_ref, vec_ref,
    wo_ref, o_ref, pick_ref, _,
    gin_ref, gbin_ref, dres1_ref, do_ref, gout_ref, sums_ref, dog_ref,
    ht_ref, dh_ref, dub_ref, dab_ref, u_ref, *, row_n, col_n,
):
    step = pl.program_id(0)
    rows, width = df_ref.shape

    @pl.when(step == 0)
    def _():
        for cut in chunks(rows):
            ht_ref[:, cut] = low_ref[cut, :].T
            dh_ref[cut, :] = dres_ref[cut, :]

    u_ref[...] = dot(df_ref[...], wff_ref[...].reshape(width, -1))
    total = 0.0
    for cut in chunks(rows):
        d_u = (u_ref[cut, :] * slope_ref[0, cut, :]).astype(BF)
        dub_ref[cut, :] = d_u
        total = total + column_sum(d_u.astype(F32))
    gbin_ref[0] = jnp.broadcast_to(total, gbin_ref.shape[1:])
    dh_ref[...] += dot(dub_ref[...], win_ref[...].reshape(width, -1), NT)
    grad = dot(ht_ref[...], dub_ref[...]).astype(BF)
    gin_ref[0, :, 0] = grad.reshape(col_n, width // col_n, -1)

    @pl.when(step == row_n - 1)
    def _():
        gain, bias, low, dog = 0.0, 0.0, 0.0, 0.0
        for cut in chunks(rows):
            d_hidden, normed = dh_ref[cut, :], normed_ref[cut, :]
            d = norm_backward(d_hidden, normed, scale_ref[cut, 0:1], vec_ref[1:2, :])
            dres1_ref[cut, :] = d
            d_low = d.astype(BF)
            dab_ref[cut, :] = d_low
            gain = gain + column_sum(d_hidden * normed)
            bias = bias + column_sum(d_hidden)
            low = low + column_sum(d_low.astype(F32))
        dh_ref[...] = dot(dab_ref[...], wo_ref[...], NT)
        for cut in chunks(rows):
            d_o = dh_ref[cut, :].astype(BF)
            pick = pick_ref[cut, :]
            is_glob = jnp.sum(pick.astype(F32), axis=1, keepdims=True) > 0.5
            dog = dog + dot(pick, d_o, TN)
            do_ref[cut, :] = jnp.where(is_glob, 0.0, dh_ref[cut, :]).astype(BF)
        dog_ref[...] = dog.astype(BF)
        sums_ref[0:1, :] = low
        sums_ref[1:2, :] = gain
        sums_ref[2:3, :] = bias
        sums_ref[3:8, :] = jnp.zeros((5, sums_ref.shape[1]), F32)
        gout_ref[...] = dot(o_ref[...], dab_ref[...], TN).astype(BF)


def vector_rows(a, row, gbin_ref, sums1_ref, sums2_ref, totals, col_n, length):
    hid, width = gbin_ref.shape[2], sums1_ref.shape[1]
    deep = width // col_n
    span = totals[0].shape[1]
    grad = gbin_ref[jnp.bitwise_xor(row, a), 0:1, :]
    lines = [jnp.concatenate([grad[:, k : k + deep]] * col_n, axis=1) for k in range(0, hid, deep)]
    lines += [sums1_ref[i : i + 1, :] for i in range(3)]
    lines += [sums2_ref[i : i + 1, :] for i in (2, 0, 1)]
    head = lax.broadcasted_iota(jnp.int32, (1, width), 1) < HDIM
    for total in totals:
        wide = jnp.concatenate([total, jnp.zeros((1, width - span), F32)], axis=1)
        if a:
            wide = pltpu.roll(wide, width - a * HDIM, 1)
        wide = jnp.where(head, wide, 0.0)
        line = wide
        for c in range(1, col_n):
            line = line + pltpu.roll(wide, c * deep, 1)
        lines.append(line)
    lines.append(jnp.zeros((length - len(lines), width), F32))
    return jnp.concatenate(lines, axis=0).astype(BF)


def glob_backward(q, do, k, v, lse, og, keep):
    count, wide = q.shape
    heads = range(0, wide, HDIM)
    lse = jnp.concatenate([lse[:, h : h + 1] for h in heads], axis=0)
    q, do = stacked(q, 0.125).astype(BF), stacked(do, 1.0)
    inner = jnp.sum(do * jnp.concatenate([og] * len(heads), axis=0), axis=1, keepdims=True)
    do = do.astype(BF)
    p = jnp.exp(dot(q, k, NT) + keep - lse)
    p = jnp.where(keep < 0.0, 0.0, p)
    ds = (p * (dot(do, v, NT) - inner)).astype(BF)
    dq = (unstacked(dot(ds, k), count) * 0.125).astype(BF)
    return dq, dot(ds, q, TN), dot(p.astype(BF), do, TN)


def entry_backward_kernel(at_ref, *refs, row_n, col_n, calls, shares, last, more):
    dqs, dks, dvs, refs = refs[:calls], refs[calls : 2 * calls], refs[2 * calls : 3 * calls], refs[3 * calls :]
    qg_ref, dog_ref, k_ref, v_ref, lse_ref, og_ref, keys_ref, refs = *refs[:7], refs[7:]
    xs, refs = refs[:4], refs[4:]
    pieces, refs = refs[: row_n * col_n], refs[row_n * col_n :]
    if last:
        before_ref, earlier_ref, gbin_ref, sums1_ref, sums2_ref, keep_ref, send_ref, dx_ref = refs
    else:
        gout_ref, keep_ref, send_ref, dx_ref, totals_ref = refs
    row, col = at_ref[0], at_ref[1]
    span = row_n * HDIM
    sizes = [x.shape[0] for x in xs]
    starts = [sum(sizes[:g]) for g in range(4)]
    own = slice(starts[1], starts[2])

    def out_rows(a):
        return send_ref if a & 1 else keep_ref

    totals = []
    for i in range(shares):
        lane = slice(i * span, (i + 1) * span)
        call = i * calls // shares
        here = slice(0, span) if calls == shares else lane
        dq_ref, dk_ref, dv_ref = dqs[call], dks[call], dvs[call]
        dqg, dkg, dvg = glob_backward(
            qg_ref[:, lane], dog_ref[:, lane], k_ref[own, lane], v_ref[own, lane],
            lse_ref[:, lane], og_ref[:, lane], keys_ref[...],
        )
        dk_own = (dk_ref[own, here].astype(F32) + dkg).astype(BF)
        dv_own = (dv_ref[own, here].astype(F32) + dvg).astype(BF)
        parts = []
        for g in range(4):
            rows = slice(starts[g], starts[g] + sizes[g])
            dk = dk_own if g == 1 else dk_ref[rows, here]
            dv = dv_own if g == 1 else dv_ref[rows, here]
            dq = dq_ref[:, here] if g == 1 else dqg if g == 3 else None
            parts.append((dq, dk, dv))
        for kind in range(3):
            grad, total = 0.0, 0.0
            for g in range(4):
                term = parts[g][kind]
                if term is not None:
                    grad = grad + dot(term, xs[g][...], TN)
                    if kind != 1:
                        total = total + column_sum(term.astype(F32))
            if kind != 1:
                totals.append(total)
            for a in range(row_n):
                at = (i * 3 + kind) * HDIM
                block = grad[a * HDIM : (a + 1) * HDIM, :].astype(BF)
                out_rows(a)[a // 2, at : at + HDIM, :] = block
        mats = []
        for b in range(col_n):
            refs_b = [pieces[a * col_n + b] for a in range(row_n)]
            mats.append([share_rows(refs_b, i, kind) for kind in range(3)])
        mats = [
            jnp.concatenate(in_order([mats[b][kind] for b in range(col_n)], col), axis=1)
            for kind in range(3)
        ]
        for g in range(4):
            rows = slice(starts[g], starts[g] + sizes[g])
            value = before_ref[rows, :] if last and i == 0 else 0.0
            for kind in range(3):
                if parts[g][kind] is not None:
                    value = value + dot(parts[g][kind], mats[kind])
            if i == 0:
                dx_ref[rows, :] = value
            else:
                dx_ref[rows, :] += value
    at = 3 * shares * HDIM
    if last:
        totals = [earlier_ref[i : i + 1, :] for i in range(more[1])] + totals
        for a in range(row_n):
            out_rows(a)[a // 2, at : at + more[0], :] = vector_rows(
                a, row, gbin_ref, sums1_ref, sums2_ref, totals, col_n, more[0]
            )
    else:
        totals.append(jnp.zeros((totals_ref.shape[0] - len(totals), span), F32))
        totals_ref[...] = jnp.concatenate(totals, axis=0)
        heads = gout_ref.shape[0] // span
        for a in range(row_n):
            for i in range(heads):
                here = (i * row_n + a) * HDIM
                out_rows(a)[a // 2, at + i * HDIM : at + (i + 1) * HDIM, :] = gout_ref[
                    here : here + HDIM, :
                ]


def attend_forward_kernel(q_ref, k_ref, v_ref, bw_ref, bg_ref, o_ref, lse_ref, *, block, glob_at):
    count, window = bw_ref.shape[0], bw_ref.shape[2]
    glob = bg_ref.shape[2]
    kg, vg = k_ref[glob_at : glob_at + glob, :], v_ref[glob_at : glob_at + glob, :]
    for i in range(count):
        rows = slice(i * block, (i + 1) * block)
        q = q_ref[rows, :]
        k, v = k_ref[i * block : i * block + window, :], v_ref[i * block : i * block + window, :]
        outs = []
        for half in (0, 1):
            qh = one_head(q, half, 0.125)
            sw = dot(qh, k, NT) + bw_ref[i]
            sg = dot(qh, kg, NT) + bg_ref[i]
            m = jnp.maximum(jnp.max(sw, axis=1, keepdims=True), jnp.max(sg, axis=1, keepdims=True))
            pw, pg = jnp.exp(sw - m), jnp.exp(sg - m)
            total = jnp.sum(pw, axis=1, keepdims=True) + jnp.sum(pg, axis=1, keepdims=True)
            inv = 1.0 / total
            o = dot((pw * inv).astype(BF), v) + dot((pg * inv).astype(BF), vg)
            outs.append((o, m + jnp.log(total)))
        low = lanes((block, PAIR))
        o_ref[rows, :] = jnp.where(low, outs[0][0], outs[1][0]).astype(BF)
        lse_ref[rows, :] = jnp.where(low, outs[0][1], outs[1][1])


def attend_backward_kernel(
    q_ref, do_ref, k_ref, v_ref, lse_ref, bw_ref, bg_ref,
    dq_ref, dk_ref, dv_ref, dk_acc, dv_acc, *, block, glob_at,
):
    count, window = bw_ref.shape[0], bw_ref.shape[2]
    glob = bg_ref.shape[2]
    dk_acc[...] = jnp.zeros_like(dk_acc)
    dv_acc[...] = jnp.zeros_like(dv_acc)
    at_glob = slice(glob_at, glob_at + glob)
    kg, vg = k_ref[at_glob, :], v_ref[at_glob, :]
    for i in range(count):
        rows = slice(i * block, (i + 1) * block)
        span = slice(i * block, i * block + window)
        q, do = q_ref[rows, :], do_ref[rows, :]
        k, v = k_ref[span, :], v_ref[span, :]
        outs = []
        for half in (0, 1):
            qh, doh = one_head(q, half, 0.125), one_head(do, half, 1.0)
            lse = lse_ref[rows, half * HDIM : half * HDIM + 1]
            pw = jnp.exp(dot(qh, k, NT) + bw_ref[i] - lse)
            pg = jnp.exp(dot(qh, kg, NT) + bg_ref[i] - lse)
            tw, tg = dot(doh, v, NT), dot(doh, vg, NT)
            inner = jnp.sum(pw * tw, axis=1, keepdims=True)
            inner = inner + jnp.sum(pg * tg, axis=1, keepdims=True)
            dsw, dsg = (pw * (tw - inner)).astype(BF), (pg * (tg - inner)).astype(BF)
            outs.append(dot(dsw, k) + dot(dsg, kg))
            dk_acc[span, :] += dot(dsw, qh, TN)
            dk_acc[at_glob, :] += dot(dsg, qh, TN)
            dv_acc[span, :] += dot(pw.astype(BF), doh, TN)
            dv_acc[at_glob, :] += dot(pg.astype(BF), doh, TN)
        low = lanes((block, PAIR))
        dq_ref[rows, :] = (jnp.where(low, outs[0], outs[1]) * 0.125).astype(BF)
    dk_ref[...] = dk_acc[...].astype(BF)
    dv_ref[...] = dv_acc[...].astype(BF)


def by_pair(rows):
    return pl.BlockSpec((rows, PAIR), lambda h: (0, h))


def whole(value):
    return pl.BlockSpec(value.shape, lambda h: (0,) * value.ndim)


def params(mebibytes):
    return pltpu.CompilerParams(vmem_limit_bytes=mebibytes * 1024 * 1024)


SCALAR = pl.BlockSpec(memory_space=pltpu.SMEM)


def once(value):
    return pl.BlockSpec(value.shape, lambda *s: (0,) * value.ndim, pipeline_mode=pl.Buffered(1))


def fixed(shape):
    return pl.BlockSpec(shape, lambda *s: (0,) * len(shape))


def hbm(*values):
    return [pltpu.with_memory_space_constraint(v, pltpu.HBM) if v.ndim > 1 else v for v in values]


def to_hbm(shapes):
    return [pltpu.HBM(v.shape, v.dtype) for v in shapes]


def cost(flops, size):
    return pl.CostEstimate(flops=flops, bytes_accessed=size, transcendentals=0)


def project(at, keep, bq, bv, xs, pieces, row_n, col_n):
    rows, glob = xs[1].shape[0], xs[3].shape[0]
    ext = sum(x.shape[0] for x in xs)
    deep = pieces[0].shape[1]
    wide = bq.shape[1]
    span = row_n * HDIM
    local = wide // span
    lane = lambda n: pl.BlockSpec((n, span), lambda i: (0, i))
    shapes = [(rows, wide), (glob, wide), (ext, wide), (ext, wide)]
    return pl.pallas_call(
        functools.partial(project_kernel, row_n=row_n, col_n=col_n),
        grid=(local,),
        in_specs=[SCALAR, once(keep), lane(1), lane(1)]
        + [once(x) for x in xs]
        + [pl.BlockSpec((3 * HDIM, deep), lambda i: (i, 0)) for _ in pieces],
        out_specs=[lane(n) for n, _ in shapes]
        + [pl.BlockSpec((3, glob, span), lambda i: (0, 0, i))],
        out_shape=to_hbm([jax.ShapeDtypeStruct(v, BF) for v in shapes])
        + [jax.ShapeDtypeStruct((3, glob, wide), F32)],
        compiler_params=params(24),
        cost_estimate=cost(6_000_000_000, 10_000_000),
        name="project",
    )(*hbm(at, keep, bq, bv, *xs, *pieces))


def mlp_forward(o_parts, at, state, pick, x, wo_raw, vec, b_inner, w_both, cot, row_n, col_n):
    rows, width = x.shape
    deep, hid = width // col_n, w_both.shape[2]
    glob = state.shape[1]
    first, last = lambda i: jnp.minimum(i, row_n - 1), lambda i: jnp.maximum(i - row_n, 0)
    sds = jax.ShapeDtypeStruct
    outs = [
        sds((rows, width), F32), sds((rows, width), BF), sds((rows, width), F32),
        sds((rows, 128), F32), sds((row_n, rows, hid), F32), sds((rows, width), F32),
        sds((rows, width), BF), sds((row_n, col_n, 2, deep, hid), BF), sds((8, width), F32),
        sds((rows, width), BF), sds((glob, width), F32), sds((glob, width), F32),
        sds((width, width), BF),
    ]
    specs = [fixed(v.shape) for v in outs]
    specs[4] = pl.BlockSpec((1, rows, hid), lambda i: (first(i), 0, 0))
    specs[7] = pl.BlockSpec((1, col_n, 1, deep, hid), lambda i: (last(i), 0, 0, 0, 0))
    small = [state, pick, x, wo_raw, vec, b_inner]
    return pl.pallas_call(
        functools.partial(mlp_forward_kernel, row_n=row_n, col_n=col_n, calls=len(o_parts)),
        grid=(2 * row_n,),
        in_specs=[once(v) for v in o_parts]
        + [SCALAR]
        + [once(v) for v in small]
        + [pl.BlockSpec((col_n, deep, hid), lambda i, k=k: (first(i), k, 0)) for k in (0, 1)]
        + [once(cot)],
        out_specs=specs,
        out_shape=to_hbm(outs),
        scratch_shapes=[
            pltpu.VMEM((row_n, rows, hid), BF),
            pltpu.VMEM((rows, width), F32),
            pltpu.VMEM((rows, width), F32),
            pltpu.VMEM((width, rows), BF),
            pltpu.VMEM((rows, hid), F32),
        ],
        compiler_params=params(48),
        cost_estimate=cost(8_000_000_000, 30_000_000),
        name="mlp_forward",
    )(*hbm(*o_parts, at, *small, w_both, w_both, cot))


def mlp_backward(d_f, slope, w_both, low, dres, normed, scale, vec, wo, o, pick, grads, row_n, col_n):
    rows, width = d_f.shape
    deep, hid = width // col_n, w_both.shape[2]
    glob = pick.shape[1]
    each = lambda n, m: pl.BlockSpec((1, n, m), lambda i: (i, 0, 0))
    kind = lambda k: pl.BlockSpec((col_n, deep, hid), lambda i: (i, k, 0))
    sds = jax.ShapeDtypeStruct
    outs = [
        sds(grads.shape, BF), sds((row_n, 8, hid), F32), sds((rows, width), F32),
        sds((rows, width), BF), sds((width, width), BF), sds((8, width), F32),
        sds((glob, width), BF),
    ]
    slot = pl.BlockSpec((1, col_n, 1, deep, hid), lambda i: (i, 0, 1, 0, 0))
    specs = [slot, each(8, hid)] + [fixed(v.shape) for v in outs[2:]]
    rest = [low, dres, normed, scale, vec, wo, o, pick]
    return pl.pallas_call(
        functools.partial(mlp_backward_kernel, row_n=row_n, col_n=col_n),
        grid=(row_n,),
        in_specs=[once(d_f), each(rows, hid), kind(0), kind(1)]
        + [once(v) for v in rest]
        + [pl.BlockSpec(memory_space=pl.ANY)],
        out_specs=specs,
        out_shape=to_hbm(outs),
        input_output_aliases={4 + len(rest): 0},
        scratch_shapes=[
            pltpu.VMEM((width, rows), BF),
            pltpu.VMEM((rows, width), F32),
            pltpu.VMEM((rows, hid), BF),
            pltpu.VMEM((rows, width), BF),
            pltpu.VMEM((rows, hid), F32),
        ],
        compiler_params=params(48),
        cost_estimate=cost(9_000_000_000, 30_000_000),
        name="mlp_backward",
    )(*hbm(d_f, slope, w_both, w_both, *rest, grads))


def entry_backward(at, parts, globs, xs, pieces, row_n, col_n, first, shares, gout=None, last=None):
    width = xs[0].shape[1]
    span = row_n * HDIM
    local = width // span
    deep = width // col_n
    ext = sum(x.shape[0] for x in xs)
    lane = lambda v: pl.BlockSpec((v.shape[0], shares * span), lambda i: (0, first // shares))
    piece = pl.BlockSpec((3 * shares * HDIM, deep), lambda i: (first // shares, 0))
    qg, dog, k_ext, v_ext, lse, og, keep = globs
    args = [p[j] for j in range(3) for p in parts]
    specs = [SCALAR] + [once(v) for v in args]
    args += globs
    specs += [lane(v) for v in globs[:-1]] + [once(keep)]
    args += xs
    specs += [once(v) for v in xs]
    args += pieces
    specs += [piece for _ in pieces]
    rest = list(last) if last else [gout]
    args += rest
    specs += [once(v) for v in rest]
    length, more = 3 * shares * HDIM, None
    if last:
        lines = last[2].shape[2] // deep + 6 + 2 * local
        more = (-(-lines // 32) * 32, 2 * (local - shares))
        length += more[0]
    else:
        length += width // row_n
    shape = jax.ShapeDtypeStruct((row_n // 2, length, width), BF)
    outs = [shape, shape, jax.ShapeDtypeStruct((ext, width), F32)]
    if not last:
        outs.append(jax.ShapeDtypeStruct((8, span), F32))
    return pl.pallas_call(
        functools.partial(
            entry_backward_kernel, row_n=row_n, col_n=col_n, calls=len(parts), shares=shares,
            last=last is not None, more=more,
        ),
        grid=(1,),
        in_specs=specs,
        out_specs=[fixed(v.shape) for v in outs],
        out_shape=to_hbm(outs),
        compiler_params=params(48),
        cost_estimate=cost(3_000_000_000 * shares, 8_000_000 * shares),
        name="entry_backward",
    )(*hbm(at, *args))


def some_pairs(rows, first):
    return pl.BlockSpec((rows, PAIR), lambda h: (0, h + first))


def attend_forward(q, k_ext, v_ext, bias_w, bias_g, glob_at, first, count):
    rows = q.shape[0]
    ext = k_ext.shape[0]
    block = bias_w.shape[1]
    wide = count * PAIR
    return pl.pallas_call(
        functools.partial(attend_forward_kernel, block=block, glob_at=glob_at),
        grid=(count,),
        in_specs=[some_pairs(rows, first), some_pairs(ext, first), some_pairs(ext, first)]
        + [whole(bias_w), whole(bias_g)],
        out_specs=[by_pair(rows), by_pair(rows)],
        out_shape=to_hbm(
            [jax.ShapeDtypeStruct((rows, wide), BF), jax.ShapeDtypeStruct((rows, wide), F32)]
        ),
        compiler_params=params(20),
        cost_estimate=pl.CostEstimate(
            flops=3_500_000_000, bytes_accessed=4_000_000, transcendentals=1_700_000
        ),
        name="attend_forward",
    )(*hbm(q, k_ext, v_ext, bias_w, bias_g))


def attend_backward(q, do, k_ext, v_ext, lse, bias_w, bias_g, glob_at, first, count, inside):
    rows = q.shape[0]
    ext = k_ext.shape[0]
    block = bias_w.shape[1]
    wide = count * PAIR
    return pl.pallas_call(
        functools.partial(attend_backward_kernel, block=block, glob_at=glob_at),
        grid=(count,),
        in_specs=[some_pairs(rows, first), some_pairs(rows, first)]
        + [some_pairs(ext, first), some_pairs(ext, first), some_pairs(rows, inside)]
        + [whole(bias_w), whole(bias_g)],
        out_specs=[by_pair(rows), by_pair(ext), by_pair(ext)],
        out_shape=to_hbm(
            [
                jax.ShapeDtypeStruct((rows, wide), BF),
                jax.ShapeDtypeStruct((ext, wide), BF),
                jax.ShapeDtypeStruct((ext, wide), BF),
            ]
        ),
        scratch_shapes=[pltpu.VMEM((ext, PAIR), F32), pltpu.VMEM((ext, PAIR), F32)],
        compiler_params=params(24),
        cost_estimate=pl.CostEstimate(
            flops=8_000_000_000, bytes_accessed=5_000_000, transcendentals=1_700_000
        ),
        name="attend_backward",
    )(*hbm(q, do, k_ext, v_ext, lse, bias_w, bias_g))


def norm_forward(resid, gain, shift_by):
    center = jnp.mean(resid, axis=1, keepdims=True)
    apart = resid - center
    scale = lax.rsqrt(jnp.mean(apart * apart, axis=1, keepdims=True) + 1e-05)
    normed = apart * scale
    return normed * gain + shift_by, normed, scale


def norm_backward(grad, normed, scale, gain):
    scaled = grad * gain
    total = jnp.mean(scaled, axis=1, keepdims=True)
    mixed = jnp.mean(scaled * normed, axis=1, keepdims=True)
    return scale * (scaled - total - normed * mixed)


def on_device(
    hidden_in, w_query, b_query, w_key, w_value, b_value, w_out, b_out, gain_attn, bias_attn,
    w_in, b_in, w_ffout, b_ffout, gain_ffn, bias_ffn, glob_pos, cotangent,
):
    row_n, col_n = lax.axis_size("row"), lax.axis_size("col")
    row_i, col_i = lax.axis_index("row"), lax.axis_index("col")
    rows = hidden_in.shape[0]
    wide, deep = w_query.shape[1], w_query.shape[0]
    hid = w_in.shape[1]
    local = wide // HDIM
    glob_row = glob_pos[0]
    glob = glob_row.shape[0]
    me = row_i * col_n + col_i
    halo = Halo(rows, row_n * col_n)
    is_prompt = me < halo.half

    own_rows = me * rows + jnp.arange(rows, dtype=jnp.int32)
    pick = (own_rows[:, None] == glob_row[None, :]).astype(BF)
    kinds = [w.T.reshape(local, 1, HDIM, deep) for w in (w_query, w_key, w_value)]
    entry = jnp.concatenate(kinds, axis=1).astype(BF).reshape(3 * wide, deep)
    x_glob = dot(pick, hidden_in, TN).astype(BF)
    x_glob = jnp.concatenate(jnp.split(x_glob, col_n, axis=1), axis=0)
    message = jnp.concatenate([entry, x_glob], axis=0)
    pieces = gather_far(message)
    x_left, x_right, hop = halo.fetch(hidden_in, is_prompt)
    ratio = hid // deep
    both = jnp.concatenate(
        [w_in, w_ffout, jnp.concatenate(jnp.split(w_out, ratio, axis=0), axis=1)], axis=0
    ).astype(BF)
    vec_row = jnp.concatenate([b_query, b_value, b_in])[None]
    vec_col = jnp.concatenate([b_out, gain_attn, bias_attn, b_ffout, gain_ffn, bias_ffn])[None]
    hop, vec_row, vec_col, both = fence(hop, vec_row, vec_col, both)
    w_both = lax.all_gather(both, ("row", "col"), axis=0)
    wo_raw = jnp.concatenate(jnp.split(w_both[:, 2 * deep :], ratio, axis=2), axis=1)
    row_vec, col_vec = {0: vec_row}, {0: vec_col}
    for bit in (1 << i for i in range((row_n - 1).bit_length())):
        row_vec.update({a ^ bit: swap(v, ("row", bit)) for a, v in list(row_vec.items())})
    for bit in (1 << i for i in range((col_n - 1).bit_length())):
        col_vec.update({b ^ bit: swap(v, ("col", bit)) for b, v in list(col_vec.items())})

    pieces = gather_near(pieces)
    names = [(a, b) for a in range(row_n) for b in range(col_n)]
    x_glob = functools.reduce(jnp.add, [pieces[k][3 * wide : 3 * wide + glob * col_n] for k in names])
    x_glob = jnp.concatenate(jnp.split(x_glob, col_n, axis=0), axis=1)
    cols = in_order([col_vec[b].reshape(6, deep) for b in range(col_n)], col_i)
    cols = jnp.pad(jnp.concatenate(cols, axis=1), ((0, 2), (0, 0)))
    row_vec = [row_vec[a][0] for a in range(row_n)]
    b_inner = jnp.stack(in_order([v[2 * wide :] for v in row_vec], row_i))[:, None, :]

    def by_share(at):
        parts = jnp.stack([v[at : at + wide].reshape(local, HDIM) for v in row_vec], axis=1)
        return parts.reshape(1, -1)

    own_at, glob_at = WIN, 2 * WIN + rows
    at = jnp.stack([row_i, col_i]).astype(jnp.int32)
    block = min(rows, WIN)
    bias_w, bias_g = bias_blocks(own_rows, halo.key_rows(me, is_prompt), glob_row, block)
    keep = jnp.where(is_prompt, 0.0, NEG) * jnp.ones((1, rows), F32)
    piece_list = [pieces[k] for k in names]
    xs = [x_left, hidden_in, x_right, x_glob]
    q, qg, k_ext, v_ext, state = project(
        at, keep, by_share(0), by_share(wide), xs, piece_list, row_n, col_n
    )

    span = row_n * HDIM
    share = span // PAIR
    rounds = [step for step in far_steps() if step != ("row", row_n // 2)] + [NEAR]
    rounds = [rounds[:-1], rounds[-1:]]
    calls = [(0, (local - 1) * share), ((local - 1) * share, share)]
    o_parts, lse_parts = [], []
    for i, (first_pair, count) in enumerate(calls):
        o_part, lse_part = attend_forward(
            q, k_ext, v_ext, bias_w, bias_g, glob_at, first_pair, count
        )
        o_parts.append(o_part)
        lse_parts.append(lse_part)
        for step in rounds[i]:
            state = merge_states(state, swap(state, step), step)
        if i == 0:
            state, q, o_parts[-1] = fence(state, q, o_part)

    (
        hidden_out, low, normed1, scale1, slope, d_resid2, d_f, ff_grads, sums2, o, og, lse_g, wo,
    ) = mlp_forward(
        o_parts, at, state, pick, hidden_in, wo_raw, cols, b_inner, w_both, cotangent, row_n, col_n
    )

    grads, grad_b_in, d_resid1, d_o, out_grads, sums1, dog = mlp_backward(
        d_f, slope, w_both, low, d_resid2, normed1, scale1, cols, wo, o, pick, ff_grads, row_n, col_n
    )
    grads = grads.reshape(row_n * col_n, 2 * deep, hid)
    grads = lax.psum_scatter(grads, ("row", "col"), scatter_dimension=0, tiled=True)[0]

    def attend_share(i, d_o):
        at_call = min(i // (local - 1), 1)
        inside = i * share - calls[at_call][0]
        return attend_backward(
            q, d_o, k_ext, v_ext, lse_parts[at_call], bias_w, bias_g, glob_at, i * share, share, inside
        )

    parts = []
    for i in range(local - 1):
        parts.append(attend_share(i, d_o))
        for step in rounds[i] if i < len(rounds) else []:
            dog = add_heads(dog, swap(dog, step), step)
        if i < local - 2:
            dog, d_o, parts[-1] = fence(dog, d_o, parts[-1])
    globs = [qg, dog, k_ext, v_ext, lse_g, og, keep]
    keep_rows, send_rows, dx, totals = entry_backward(
        at, parts, globs, xs, piece_list, row_n, col_n, 0, local - 1, gout=out_grads
    )
    near = near_pieces(at, keep_rows, swap(send_rows, NEAR), col_n)
    near, d_o = fence(near, d_o)
    part = attend_share(local - 1, d_o)
    keep_rows, send_rows, dx = entry_backward(
        at, [part], globs, xs, piece_list, row_n, col_n, local - 1, 1,
        last=(dx, totals, grad_b_in, sums1, sums2),
    )
    entry_first = far_sum(near)
    near = near_pieces(at, keep_rows, swap(send_rows, NEAR), col_n)
    near, grads, entry_first = fence(near, grads, entry_first)
    grads = lax.psum(grads, "seq")
    entry_last = far_sum(near)
    grad_entry, dx = fence(jnp.concatenate([entry_first, entry_last], axis=0), dx)
    grad_entry = seq_sum(grad_entry)
    _, grads = fence(grad_entry, grads)
    grads = grads.astype(F32)
    entry_first, entry_last = grad_entry[: entry_first.shape[0]], grad_entry[entry_first.shape[0] :]

    dx_glob = group_sum(dx[glob_at:], lambda a, b, step: a + b)
    first, last = halo.give(dx[:WIN], dx[own_at + rows : glob_at], is_prompt)
    grad_x = d_resid1 + dx[own_at : own_at + rows]
    grad_x = grad_x + lax.dot_general(
        pick.astype(F32), dx_glob, NN, precision=lax.Precision.HIGHEST, preferred_element_type=F32
    )
    size = first.shape[0]
    grad_x = jnp.concatenate([grad_x[:size] + first, grad_x[size:]], axis=0)
    grad_x = jnp.concatenate([grad_x[:-size], grad_x[-size:] + last], axis=0)

    cut = 3 * (local - 1) * HDIM
    by_kind = jnp.concatenate([entry_first[:cut], entry_last[: 3 * HDIM]], axis=0)
    by_kind = by_kind.reshape(local, 3, HDIM, deep)
    grad_out = entry_first[cut:]
    tail = entry_last[3 * HDIM :]
    b_rows = hid // deep
    bias_rows = tail[b_rows + 6 : b_rows + 6 + 2 * local, :HDIM].reshape(local, 2, HDIM)
    col_vectors = tail[b_rows : b_rows + 6]
    return (
        hidden_out,
        grad_x,
        by_kind[:, 0].reshape(wide, deep).T,
        bias_rows[:, 0].reshape(wide),
        by_kind[:, 1].reshape(wide, deep).T,
        by_kind[:, 2].reshape(wide, deep).T,
        bias_rows[:, 1].reshape(wide),
        grad_out,
        col_vectors[0],
        col_vectors[1],
        col_vectors[2],
        grads[deep:],
        tail[:b_rows].reshape(-1),
        grads[:deep],
        col_vectors[3],
        col_vectors[4],
        col_vectors[5],
    )


def solution(mesh):
    tokens = P(("seq", "row", "col"), None)
    both, row, col = P("col", "row"), P("row"), P("col")
    in_specs = (
        tokens, both, row, both, both, row, P("row", "col"), col, col, col, both, row, both, col,
        col, col, P("seq", None), tokens,
    )
    out_specs = (
        tokens, tokens, both, row, both, both, row, P("row", "col"), col, col, col, both, row,
        both, col, col, col,
    )
    return jax.shard_map(
        on_device, mesh=mesh, in_specs=in_specs, out_specs=out_specs, check_vma=False
    )
```

```python
import functools
import math

import jax
import jax.numpy as jnp
from jax import lax
from jax.experimental import pallas as pl
from jax.experimental.pallas import tpu as pltpu
from jax.sharding import PartitionSpec as P

D = 768
HDIM = 64
WIN = 256
PLEN = 2048
LC = 256
PAIR = 2 * HDIM
FAR = -(1 << 20)
BF = jnp.bfloat16
F32 = jnp.float32
NEG = -1e30

NN = (((1,), (0,)), ((), ()))
NT = (((1,), (1,)), ((), ()))
TN = (((0,), (0,)), ((), ()))


def dot(a, b, dims=NN):
    return lax.dot_general(a, b, dims, preferred_element_type=F32)


def swap(value, step):
    axis, bit = step
    size = lax.axis_size(axis)
    return lax.ppermute(value, axis, [(i, i ^ bit) for i in range(size)])


def far_steps():
    rows, cols = lax.axis_size("row"), lax.axis_size("col")
    steps, bit = [], 1
    while bit < cols:
        steps.append(("col", bit))
        bit *= 2
    bit = 2
    while bit < rows:
        steps.append(("row", bit))
        bit *= 2
    return steps


NEAR = ("row", 1)


def move(name, step):
    axis, bit = step
    return (name[0] ^ bit, name[1]) if axis == "row" else (name[0], name[1] ^ bit)


def fence(*values):
    return lax.optimization_barrier(values)


def swap_both(value, row_bit, col_bit):
    rows, cols = lax.axis_size("row"), lax.axis_size("col")
    pairs = [
        (r * cols + c, (r ^ row_bit) * cols + (c ^ col_bit))
        for r in range(rows)
        for c in range(cols)
    ]
    return lax.ppermute(value, ("row", "col"), pairs)


def far_names():
    rows, cols = lax.axis_size("row"), lax.axis_size("col")
    return [(a, b) for a in range(0, rows, 2) for b in range(cols) if (a, b) != (0, 0)]


def gather_far(own):
    far = far_steps()
    pieces = {(0, 0): own}
    if len(far) != 2:
        return pieces | {name: swap_both(own, *name) for name in far_names()}
    first, second = far
    a, b = swap(own, first), swap(own, second)
    half = own.shape[0] // 2
    corner = [swap(b[:half], first), swap(a[half:], second)]
    at_first, at_second = move((0, 0), first), move((0, 0), second)
    return pieces | {
        at_first: a,
        at_second: b,
        move(at_first, second): jnp.concatenate(corner, axis=0),
    }


def gather_near(pieces):
    return pieces | {move(k, NEAR): swap(v, NEAR) for k, v in pieces.items()}


def in_order(parts, me):
    bit = 1
    while bit < len(parts):
        odd = (me & bit) != 0
        parts = [jnp.where(odd, parts[t ^ bit], parts[t]) for t in range(len(parts))]
        bit *= 2
    return parts


def near_kernel(at_ref, keep_ref, got_ref, *out_refs, col_n):
    for half in range(keep_ref.shape[0]):
        near = keep_ref[half].astype(F32) + got_ref[half].astype(F32)
        for b, part in enumerate(columns(near, col_n, at_ref[1])):
            out = out_refs[half * col_n + b]
            out[...] = part.astype(out.dtype)


def near_pieces(at, keep, got, col_n):
    halves, length, width = keep.shape
    count = halves * col_n
    piece = (length, width // col_n)
    shapes = [jax.ShapeDtypeStruct(piece, BF if i else F32) for i in range(count)]
    return pl.pallas_call(
        functools.partial(near_kernel, col_n=col_n),
        in_specs=[SCALAR] + [pl.BlockSpec(memory_space=pltpu.VMEM)] * 2,
        out_shape=to_hbm(shapes),
        compiler_params=params(24),
        name="near_pieces",
    )(*hbm(at, keep, got))


def far_sum(parts):
    cols = lax.axis_size("col")
    total = parts[0]
    for a, b in far_names():
        total = total + swap_both(parts[a // 2 * cols + b], a, b).astype(F32)
    return total


def seq_turn(part, k):
    count = lax.axis_size("seq")
    return lax.ppermute(part, "seq", [(i, (i + k) % count) for i in range(count)])


def seq_scatter(value):
    count, me = lax.axis_size("seq"), lax.axis_index("seq")
    parts = value.astype(BF).reshape((count, value.shape[0] // count) + value.shape[1:])
    total = lax.dynamic_index_in_dim(parts, me, 0, keepdims=False).astype(F32)
    for k in range(1, count):
        part = lax.dynamic_index_in_dim(parts, (me + k) % count, 0, keepdims=False)
        total = total + seq_turn(part, k).astype(F32)
    return total.astype(BF)


def seq_gather(own):
    count, me = lax.axis_size("seq"), lax.axis_index("seq")
    held = jnp.stack([own] + [seq_turn(own, k) for k in range(1, count)])
    return [lax.dynamic_index_in_dim(held, (me - i) % count, 0, keepdims=False) for i in range(count)]


def group_sum(value, merge):
    for step in far_steps() + [NEAR]:
        value = merge(value, swap(value, step), step)
    return value


def shift(value, pairs):
    return lax.ppermute(value, ("row", "col"), pairs) if pairs else jnp.zeros_like(value)


class Halo:
    def __init__(self, rows, devices):
        self.rows = rows
        self.n = devices
        self.half = PLEN // rows
        self.block = min(rows, WIN)
        self.steps = WIN // self.block
        self.wide = rows >= 2 * WIN

    def pairs_left(self, t):
        return [(j - t, j) for j in range(self.half) if j >= t]

    def pairs_right(self, t):
        return [(j + t, j) for j in range(self.half) if j + t < self.half]

    def pairs_mates(self, t):
        return [(self.mate(j, t), j) for j in range(self.half, self.n)]

    def mate(self, j, t):
        base = j - j % self.steps
        return base + (j - base + t) % self.steps

    def tree(self, t):
        source = self.half - self.steps + t
        rounds, bit = [[(source, source + self.half)]], 1
        have = [source + self.half]
        while len(have) < self.n - self.half:
            rounds.append([(d, d ^ bit) for d in have])
            have += [d ^ bit for d in have]
            bit *= 2
        return rounds

    def fetch(self, own, is_prompt):
        first, last = own[: self.block], own[-self.block :]
        left, right, tail = [], [], []
        for t in range(self.steps, 0, -1):
            at = self.steps - t
            rounds = self.tree(at)
            if self.steps == 1:
                left.append(shift(last, self.pairs_left(t) + rounds[0]))
                mixed = jnp.where(is_prompt, first, left[0])
                right.append(shift(mixed, self.pairs_right(t) + rounds[1]))
                held = left[0] + jnp.where(is_prompt, jnp.zeros((), BF), right[0])
                rounds = rounds[2:]
            else:
                left.append(shift(last, self.pairs_left(t)))
                right.append(shift(first, self.pairs_right(at + 1)))
                held = shift(last, rounds[0])
                rounds = rounds[1:]
            for pairs in rounds:
                held = held + shift(held, pairs)
            tail.append(held)
        hop = left[0]
        left = [jnp.where(is_prompt, a, b) for a, b in zip(left, tail)]
        if self.wide:
            right = [jnp.where(is_prompt, a, b) for a, b in zip(right, tail)]
        elif self.steps > 1:
            mates = [shift(own, self.pairs_mates(t)) for t in range(1, self.steps)]
            right = [jnp.where(is_prompt, a, b) for a, b in zip(right, mates)] + right[len(mates) :]
        return jnp.concatenate(left, axis=0), jnp.concatenate(right, axis=0), hop

    def give(self, left, right, is_prompt):
        block = self.block

        def cut(value):
            return [value[t * block : (t + 1) * block] for t in range(self.steps)]

        def back(value, pairs):
            return shift(value, [(b, a) for a, b in pairs]).astype(F32)

        zero = jnp.zeros((), F32)
        left, right = cut(left), cut(right)
        first = jnp.zeros((block, left[0].shape[1]), F32)
        last = first
        for i, t in enumerate(range(self.steps, 0, -1)):
            last = last + back(left[i].astype(BF), self.pairs_left(t))
        for i, t in enumerate(range(1, self.steps + 1)):
            first = first + back(right[i].astype(BF), self.pairs_right(t))
        for t in range(self.steps):
            held = left[t] + right[t] if self.wide else left[t]
            held = jnp.where(is_prompt, zero, held)
            rounds = self.tree(t)
            for pairs in reversed(rounds[1:]):
                held = held + back(held.astype(BF), pairs)
            last = last + back(held.astype(BF), rounds[0])
        if not self.wide:
            for t in range(1, self.steps):
                first = first + back(right[t - 1].astype(BF), self.pairs_mates(t))
        return first, last

    def key_rows(self, me, is_prompt):
        near = jnp.arange(WIN, dtype=jnp.int32)
        start = me * self.rows
        left = start - WIN + near
        left = jnp.where(left < 0, FAR, left)
        left = jnp.where(is_prompt, left, PLEN - WIN + near)
        right = start + self.rows + near
        right = jnp.where(right < PLEN, right, FAR)
        if self.wide:
            other = PLEN - WIN + near
        elif self.steps > 1:
            parts = [
                (me - me % self.steps + (me % self.steps + t) % self.steps) * self.rows
                + jnp.arange(self.rows, dtype=jnp.int32)
                for t in range(1, self.steps)
            ]
            other = jnp.concatenate(parts + [jnp.full((self.rows,), FAR, jnp.int32)])
        else:
            other = jnp.full((WIN,), FAR, jnp.int32)
        right = jnp.where(is_prompt, right, other)
        own = start + jnp.arange(self.rows, dtype=jnp.int32)
        return jnp.concatenate([left, own, right])


def place_of(index):
    after = index - PLEN
    return jnp.where(index < PLEN, index, PLEN + after % LC)


def bias_blocks(query_rows, key_rows, glob_row, block):
    count = query_rows.shape[0] // block
    query = query_rows.reshape(count, block, 1)
    keys = jnp.stack([key_rows[i * block : i * block + 2 * WIN + block] for i in range(count)])
    keys = keys[:, None, :]
    near = (jnp.abs(place_of(query) - keys) <= WIN) & (keys < PLEN) & (keys >= 0)
    same = (query >= PLEN) & (keys >= PLEN) & ((query - PLEN) // LC == (keys - PLEN) // LC)
    window = jnp.where(near | same, 0.0, NEG).astype(F32)
    beyond = jnp.abs(place_of(query) - glob_row[None, None, :]) > WIN
    return window, jnp.where(beyond, 0.0, NEG).astype(F32)


def lanes(shape):
    return lax.broadcasted_iota(jnp.int32, shape, 1) < HDIM


def one_head(value, half, scale):
    keep = lanes(value.shape)
    keep = keep if half == 0 else ~keep
    return (jnp.where(keep, value.astype(F32), 0.0) * scale).astype(BF)


def stacked(value, scale):
    head = lax.broadcasted_iota(jnp.int32, value.shape, 1) // HDIM
    value = value.astype(F32) * scale
    parts = [jnp.where(head == h, value, 0.0) for h in range(value.shape[1] // HDIM)]
    return jnp.concatenate(parts, axis=0)


def unstacked(value, count):
    shape = (count, value.shape[1])
    head = lax.broadcasted_iota(jnp.int32, shape, 1) // HDIM
    out = jnp.zeros(shape, F32)
    for h in range(value.shape[0] // count):
        out = jnp.where(head == h, value[h * count : (h + 1) * count, :], out)
    return out


def glob_state(q, k, v, keep):
    count, wide = q.shape
    s = dot(stacked(q, 0.125).astype(BF), k, NT) + keep
    m = jnp.max(s, axis=1, keepdims=True)
    p = jnp.exp(s - m)
    total = jnp.sum(p, axis=1, keepdims=True)
    o = dot(p.astype(BF), v)
    return [unstacked(jnp.broadcast_to(t, o.shape), count) for t in (o, m, total)]


def share_rows(refs, share, kind):
    at = (share * 3 + kind) * HDIM
    return jnp.concatenate([r[at : at + HDIM, :] for r in refs], axis=0)


def columns(value, count, me):
    size = value.shape[1] // count
    return in_order([value[:, c * size : (c + 1) * size] for c in range(count)], me)


def pack_kernel(at_ref, glob_ref, x_ref, wq_ref, wk_ref, wv_ref, out_ref, *, col_n, glob_at):
    rows, width = x_ref.shape
    deep, local = width // col_n, wq_ref.shape[0] // HDIM
    for kind, w_ref in enumerate((wq_ref, wk_ref, wv_ref)):
        for i in range(local):
            at = (i * 3 + kind) * HDIM
            out_ref[at : at + HDIM, :] = w_ref[i * HDIM : (i + 1) * HDIM, :].astype(BF)
    glob = glob_ref.shape[1]
    row = lax.broadcasted_iota(jnp.int32, (rows, glob), 0) + at_ref[3]
    pick = (row == glob_ref[...]).astype(F32).astype(BF)
    own = dot(pick, x_ref[...], TN).astype(BF)
    for c in range(col_n):
        at = glob_at + c * glob
        out_ref[at : at + glob, :] = own[:, c * deep : (c + 1) * deep]


def pack(at, glob_row, x, w_query, w_key, w_value, col_n):
    wide, deep = w_query.shape
    more = glob_row.shape[1] * col_n
    glob_at = -(-3 * wide // more) * more
    return pl.pallas_call(
        functools.partial(pack_kernel, col_n=col_n, glob_at=glob_at),
        in_specs=[SCALAR] + [pl.BlockSpec(memory_space=pltpu.VMEM)] * 5,
        out_shape=pltpu.HBM((glob_at + more, deep), BF),
        compiler_params=params(16),
        name="pack",
    )(*hbm(at, glob_row, x, w_query, w_key, w_value))


def project_kernel(at_ref, *refs, row_n, col_n):
    vecs, refs = refs[:row_n], refs[row_n:]
    (left_ref, own_ref, right_ref), refs = refs[:3], refs[3:]
    pieces, refs = refs[: row_n * col_n], refs[row_n * col_n :]
    extra, refs = refs[: row_n * col_n], refs[row_n * col_n :]
    q_ref, qg_ref, k_ref, v_ref, state_ref, xg_ref = refs
    share, col = pl.program_id(0), at_ref[1]
    span = row_n * HDIM
    glob = xg_ref.shape[0]
    total = functools.reduce(jnp.add, [r[...].astype(F32) for r in extra])
    parts = [total[c * glob : (c + 1) * glob, :] for c in range(col_n)]
    xg = jnp.concatenate(parts, axis=1).astype(BF)
    xg_ref[...] = xg
    lines = [r[pl.ds(share, 1), :] for r in vecs]
    bias_q = jnp.concatenate([v[:, :HDIM] for v in lines], axis=1)
    bias_v = jnp.concatenate([v[:, HDIM : 2 * HDIM] for v in lines], axis=1)
    mats = []
    for b in range(col_n):
        refs_b = [pieces[a * col_n + b] for a in range(row_n)]
        mats.append(jnp.concatenate([share_rows(refs_b, 0, kind) for kind in range(3)], axis=0))

    at = 0
    for g, x in enumerate((left_ref[...], own_ref[...], right_ref[...], xg)):
        rows = slice(at, at + x.shape[0])
        at += x.shape[0]
        first = 0 if g in (1, 3) else span
        total = 0.0
        for part, mat in zip(columns(x, col_n, col), mats):
            total = total + dot(part, mat[first:, :], NT)
        k_ref[rows, :] = total[:, span - first : 2 * span - first].astype(BF)
        v_ref[rows, :] = (total[:, 2 * span - first :] + bias_v).astype(BF)
        if first == 0:
            out = q_ref if g == 1 else qg_ref
            out[...] = (total[:, :span] + bias_q).astype(BF)
    rows = slice(left_ref.shape[0], left_ref.shape[0] + own_ref.shape[0])
    keep = jnp.where(at_ref[2] > 0, 0.0, NEG)
    state = glob_state(qg_ref[...], k_ref[rows, :], v_ref[rows, :], keep)
    for i in range(3):
        state_ref[i] = state[i]


def swap_heads(value, bit):
    blocks = [value[..., i * PAIR : (i + 1) * PAIR] for i in range(value.shape[-1] // PAIR)]
    if bit == 1:
        return [pltpu.roll(v, HDIM, v.ndim - 1) for v in blocks]
    return [blocks[i ^ (bit // 2)] for i in range(len(blocks))]


def merge_kernel(one_ref, two_ref, out_ref, *, bit):
    for i in range(one_ref.shape[2] // PAIR):
        span = slice(i * PAIR, (i + 1) * PAIR)
        o1, m1, l1 = [one_ref[j, :, span] for j in range(3)]
        o2, m2, l2 = [swap_heads(two_ref[j], bit)[i] for j in range(3)]
        top = jnp.maximum(m1, m2)
        a, b = jnp.exp(m1 - top), jnp.exp(m2 - top)
        out_ref[0, :, span] = o1 * a + o2 * b
        out_ref[1, :, span] = top
        out_ref[2, :, span] = l1 * a + l2 * b


def add_heads_kernel(one_ref, two_ref, out_ref, *, bit):
    for i, block in enumerate(swap_heads(two_ref[...].astype(F32), bit)):
        span = slice(i * PAIR, (i + 1) * PAIR)
        out_ref[:, span] = (one_ref[:, span].astype(F32) + block).astype(BF)


def head_bit(step):
    return step[1] if step[0] == "row" else 0


def merge_states(one, two, step):
    return pl.pallas_call(
        functools.partial(merge_kernel, bit=head_bit(step)),
        out_shape=jax.ShapeDtypeStruct(one.shape, one.dtype),
        name="merge_states",
    )(one, two)


def add_heads(one, two, step):
    return pl.pallas_call(
        functools.partial(add_heads_kernel, bit=head_bit(step)),
        out_shape=jax.ShapeDtypeStruct(one.shape, one.dtype),
        name="add_heads",
    )(one, two)


def chunks(rows):
    size = min(rows, 128)
    return [slice(i, i + size) for i in range(0, rows, size)]


def gelu_parts(u):
    density = jnp.exp(u * u * -0.5)
    t = 1.0 / (1.0 + 0.2316418863 * jnp.abs(u))
    poly = 1.061405429 * t - 1.453152027
    poly = poly * t + 1.421413741
    poly = poly * t - 0.284496736
    poly = poly * t + 0.254829592
    tail = 0.5 * poly * t * density
    phi = jnp.where(u >= 0.0, 1.0 - tail, tail)
    return u * phi, phi + u * density * 0.3989422804014327


def column_sum(value):
    return jnp.sum(value, axis=0, keepdims=True)


def mlp_kernel(*refs, row_n, col_n, calls):
    o_parts, refs = refs[:calls], refs[calls:]
    vecs, refs = refs[:row_n], refs[row_n:]
    col_vecs, refs = refs[:col_n], refs[col_n:]
    (
        at_ref, state_ref, pick_ref, x_ref, cot_ref, wraw_ref, win_ref, wff_ref,
        out_ref, grads_ref, gbin_ref, dres_ref, do_ref, gout_ref, sums_ref, dog_ref, og_ref, lse_ref,
        vec_ref, bin_ref, wo_ref, o_ref, low_ref, lowt_ref, act_ref, slope_ref, f_ref, hid_ref,
        normed_ref, scale_ref, df_ref, dft_ref, u_ref, du_ref,
    ) = refs
    step = pl.program_id(0)
    rows, width = x_ref.shape
    deep, local, hid = width // col_n, width // (row_n * HDIM), win_ref.shape[2]

    @pl.when(step == 0)
    def _():
        parts = in_order([v[...] for v in col_vecs], at_ref[1])
        vec_ref[...] = jnp.concatenate(parts, axis=1)
        for r, part in enumerate(in_order([v[...] for v in vecs], at_ref[0])):
            lines = [part[local + j : local + j + 1, :] for j in range(hid // 128)]
            bin_ref[r] = jnp.broadcast_to(jnp.concatenate(lines, axis=1), bin_ref.shape[1:])
        count = wraw_ref.shape[1]
        unit = math.gcd(HDIM, count)
        for a in range(row_n):
            for c in range(col_n):
                raw = wraw_ref[jnp.bitwise_xor(at_ref[0], a) * col_n + c]
                for row in range(0, local * HDIM, unit):
                    to = (row // HDIM * row_n + a) * HDIM + row % HDIM
                    part, off = row // count, row % count
                    wo_ref[to : to + unit, c * deep : (c + 1) * deep] = raw[
                        off : off + unit, part * deep : (part + 1) * deep
                    ]
        og = state_ref[0] / state_ref[2]
        og_ref[...] = og
        lse_ref[...] = state_ref[1] + jnp.log(state_ref[2])
        og = og.astype(BF)
        for cut in chunks(rows):
            pick = pick_ref[cut, :]
            is_glob = jnp.sum(pick.astype(F32), axis=1, keepdims=True) > 0.5
            o = jnp.concatenate([r[cut, :] for r in o_parts], axis=1)
            o_ref[cut, :] = jnp.where(is_glob, dot(pick, og), o.astype(F32)).astype(BF)
        f_ref[...] = dot(o_ref[...], wo_ref[...])
        for cut in chunks(rows):
            resid = x_ref[cut, :].astype(F32) + f_ref[cut, :] + vec_ref[0:1, :]
            hidden, normed, scale = norm_forward(resid, vec_ref[1:2, :], vec_ref[2:3, :])
            hid_ref[cut, :] = hidden
            low = hidden.astype(BF)
            low_ref[cut, :] = low
            lowt_ref[:, cut] = low.T
            normed_ref[cut, :] = normed
            scale_ref[cut, :] = jnp.broadcast_to(scale, (scale.shape[0], scale_ref.shape[1]))
        f_ref[...] = jnp.zeros_like(f_ref)

    @pl.when(step < row_n)
    def _():
        u_ref[...] = dot(low_ref[...], win_ref[...].reshape(width, -1))
        for cut in chunks(rows):
            act, slope = gelu_parts(u_ref[cut, :] + bin_ref[step, 0:1, :])
            act_ref[step, cut, :] = act.astype(BF)
            slope_ref[step, cut, :] = slope
        f_ref[...] += dot(act_ref[step], wff_ref[...].reshape(width, -1), NT)

    @pl.when(step == row_n - 1)
    def _():
        gain, bias, low = 0.0, 0.0, 0.0
        for cut in chunks(rows):
            resid = hid_ref[cut, :] + f_ref[cut, :] + vec_ref[3:4, :]
            out, normed, scale = norm_forward(resid, vec_ref[4:5, :], vec_ref[5:6, :])
            out_ref[cut, :] = out
            g = cot_ref[cut, :].astype(F32)
            d = norm_backward(g, normed, scale, vec_ref[4:5, :])
            f_ref[cut, :] = d
            d_low = d.astype(BF)
            df_ref[cut, :] = d_low
            dft_ref[:, cut] = d_low.T
            gain = gain + column_sum(g * normed)
            bias = bias + column_sum(g)
            low = low + column_sum(d_low.astype(F32))
        sums_ref[3:4, :] = low
        sums_ref[4:5, :] = gain
        sums_ref[5:6, :] = bias
        sums_ref[6:8, :] = jnp.zeros((2, width), F32)

    @pl.when(step >= row_n)
    def _():
        now = step - row_n
        u_ref[...] = dot(df_ref[...], wff_ref[...].reshape(width, -1))
        grad = dot(dft_ref[...], act_ref[now]).astype(BF)
        grads_ref[0, :, 0] = grad.reshape(col_n, deep, -1)
        total = 0.0
        for cut in chunks(rows):
            d_u = (u_ref[cut, :] * slope_ref[now, cut, :]).astype(BF)
            du_ref[cut, :] = d_u
            total = total + column_sum(d_u.astype(F32))
        gbin_ref[0] = jnp.broadcast_to(total, gbin_ref.shape[1:])
        f_ref[...] += dot(du_ref[...], win_ref[...].reshape(width, -1), NT)
        grad = dot(lowt_ref[...], du_ref[...]).astype(BF)
        grads_ref[0, :, 1] = grad.reshape(col_n, deep, -1)

    @pl.when(step == 2 * row_n - 1)
    def _():
        gain, bias, low, dog = 0.0, 0.0, 0.0, 0.0
        for cut in chunks(rows):
            d_hidden, normed = f_ref[cut, :], normed_ref[cut, :]
            d = norm_backward(d_hidden, normed, scale_ref[cut, 0:1], vec_ref[1:2, :])
            dres_ref[cut, :] = d
            d_low = d.astype(BF)
            df_ref[cut, :] = d_low
            gain = gain + column_sum(d_hidden * normed)
            bias = bias + column_sum(d_hidden)
            low = low + column_sum(d_low.astype(F32))
        f_ref[...] = dot(df_ref[...], wo_ref[...], NT)
        for cut in chunks(rows):
            d_o = f_ref[cut, :].astype(BF)
            pick = pick_ref[cut, :]
            is_glob = jnp.sum(pick.astype(F32), axis=1, keepdims=True) > 0.5
            dog = dog + dot(pick, d_o, TN)
            do_ref[cut, :] = jnp.where(is_glob, 0.0, f_ref[cut, :]).astype(BF)
        dog_ref[...] = dog.astype(BF)
        sums_ref[0:1, :] = low
        sums_ref[1:2, :] = gain
        sums_ref[2:3, :] = bias
        gout_ref[...] = dot(o_ref[...], df_ref[...], TN).astype(BF)


def vector_rows(a, row, gbin_ref, sums_ref, totals, col_n, length):
    hid, width = gbin_ref.shape[2], sums_ref.shape[1]
    deep = width // col_n
    span = totals[0].shape[1]
    grad = gbin_ref[jnp.bitwise_xor(row, a), 0:1, :]
    lines = [jnp.concatenate([grad[:, k : k + deep]] * col_n, axis=1) for k in range(0, hid, deep)]
    lines += [sums_ref[i : i + 1, :] for i in range(6)]
    head = lax.broadcasted_iota(jnp.int32, (1, width), 1) < HDIM
    for total in totals:
        wide = jnp.concatenate([total, jnp.zeros((1, width - span), F32)], axis=1)
        if a:
            wide = pltpu.roll(wide, width - a * HDIM, 1)
        wide = jnp.where(head, wide, 0.0)
        line = wide
        for c in range(1, col_n):
            line = line + pltpu.roll(wide, c * deep, 1)
        lines.append(line)
    lines.append(jnp.zeros((length - len(lines), width), F32))
    return jnp.concatenate(lines, axis=0).astype(BF)


def glob_backward(q, do, k, v, lse, og, keep):
    count, wide = q.shape
    heads = range(0, wide, HDIM)
    lse = jnp.concatenate([lse[:, h : h + 1] for h in heads], axis=0)
    q, do = stacked(q, 0.125).astype(BF), stacked(do, 1.0)
    inner = jnp.sum(do * jnp.concatenate([og] * len(heads), axis=0), axis=1, keepdims=True)
    do = do.astype(BF)
    p = jnp.exp(dot(q, k, NT) + keep - lse)
    p = jnp.where(keep < 0.0, 0.0, p)
    ds = (p * (dot(do, v, NT) - inner)).astype(BF)
    dq = (unstacked(dot(ds, k), count) * 0.125).astype(BF)
    return dq, dot(ds, q, TN), dot(p.astype(BF), do, TN)


def entry_backward_kernel(at_ref, *refs, row_n, col_n, calls, shares, last, more):
    dqs, dks, dvs, refs = refs[:calls], refs[calls : 2 * calls], refs[2 * calls : 3 * calls], refs[3 * calls :]
    qg_ref, dog_ref, k_ref, v_ref, lse_ref, og_ref, keys_ref, refs = *refs[:7], refs[7:]
    xs, refs = refs[:4], refs[4:]
    pieces, refs = refs[: row_n * col_n], refs[row_n * col_n :]
    if last:
        before_ref, earlier_ref, gbin_ref, sums_ref, keep_ref, send_ref, dx_ref = refs
    else:
        gout_ref, keep_ref, send_ref, dx_ref, totals_ref = refs
    row, col = at_ref[0], at_ref[1]
    span = row_n * HDIM
    sizes = [x.shape[0] for x in xs]
    starts = [sum(sizes[:g]) for g in range(4)]
    own = slice(starts[1], starts[2])

    def out_rows(a):
        return send_ref if a & 1 else keep_ref

    totals = []
    for i in range(shares):
        lane = slice(i * span, (i + 1) * span)
        call = i * calls // shares
        here = slice(0, span) if calls == shares else lane
        dq_ref, dk_ref, dv_ref = dqs[call], dks[call], dvs[call]
        dqg, dkg, dvg = glob_backward(
            qg_ref[:, lane], dog_ref[:, lane], k_ref[own, lane], v_ref[own, lane],
            lse_ref[:, lane], og_ref[:, lane], keys_ref[...],
        )
        dk_own = (dk_ref[own, here].astype(F32) + dkg).astype(BF)
        dv_own = (dv_ref[own, here].astype(F32) + dvg).astype(BF)
        parts = []
        for g in range(4):
            rows = slice(starts[g], starts[g] + sizes[g])
            dk = dk_own if g == 1 else dk_ref[rows, here]
            dv = dv_own if g == 1 else dv_ref[rows, here]
            dq = dq_ref[:, here] if g == 1 else dqg if g == 3 else None
            parts.append((dq, dk, dv))
        for kind in range(3):
            grad, total = 0.0, 0.0
            for g in range(4):
                term = parts[g][kind]
                if term is not None:
                    grad = grad + dot(term, xs[g][...], TN)
                    if kind != 1:
                        total = total + column_sum(term.astype(F32))
            if kind != 1:
                totals.append(total)
            for a in range(row_n):
                at = (i * 3 + kind) * HDIM
                block = grad[a * HDIM : (a + 1) * HDIM, :].astype(BF)
                out_rows(a)[a // 2, at : at + HDIM, :] = block
        mats = []
        for b in range(col_n):
            refs_b = [pieces[a * col_n + b] for a in range(row_n)]
            mats.append([share_rows(refs_b, i, kind) for kind in range(3)])
        mats = [
            jnp.concatenate(in_order([mats[b][kind] for b in range(col_n)], col), axis=1)
            for kind in range(3)
        ]
        for g in range(4):
            rows = slice(starts[g], starts[g] + sizes[g])
            value = before_ref[rows, :] if last and i == 0 else 0.0
            for kind in range(3):
                if parts[g][kind] is not None:
                    value = value + dot(parts[g][kind], mats[kind])
            if i == 0:
                dx_ref[rows, :] = value
            else:
                dx_ref[rows, :] += value
    at = 3 * shares * HDIM
    if last:
        totals = [earlier_ref[i : i + 1, :] for i in range(more[1])] + totals
        for a in range(row_n):
            out_rows(a)[a // 2, at : at + more[0], :] = vector_rows(
                a, row, gbin_ref, sums_ref, totals, col_n, more[0]
            )
    else:
        totals.append(jnp.zeros((totals_ref.shape[0] - len(totals), span), F32))
        totals_ref[...] = jnp.concatenate(totals, axis=0)
        heads = gout_ref.shape[0] // span
        for a in range(row_n):
            for i in range(heads):
                here = (i * row_n + a) * HDIM
                out_rows(a)[a // 2, at + i * HDIM : at + (i + 1) * HDIM, :] = gout_ref[
                    here : here + HDIM, :
                ]


def both_heads(value, scale):
    return jnp.concatenate([one_head(value, half, scale) for half in (0, 1)], axis=0)


def apart(value):
    size = value.shape[0] // 2
    return jnp.where(lanes((size, value.shape[1])), value[:size], value[size:])


def attend_forward_kernel(q_ref, k_ref, v_ref, bw_ref, bg_ref, o_ref, lse_ref, *, block, glob_at):
    count, window = bw_ref.shape[0], bw_ref.shape[2]
    glob = bg_ref.shape[2]
    kg, vg = k_ref[glob_at : glob_at + glob, :], v_ref[glob_at : glob_at + glob, :]
    for i in range(count):
        rows = slice(i * block, (i + 1) * block)
        span = slice(i * block, i * block + window)
        k, v = k_ref[span, :], v_ref[span, :]
        qs = both_heads(q_ref[rows, :], 0.125)
        bw, bg = bw_ref[i], bg_ref[i]
        sw = dot(qs, k, NT) + jnp.concatenate([bw, bw], axis=0)
        sg = dot(qs, kg, NT) + jnp.concatenate([bg, bg], axis=0)
        m = jnp.maximum(jnp.max(sw, axis=1, keepdims=True), jnp.max(sg, axis=1, keepdims=True))
        pw, pg = jnp.exp(sw - m), jnp.exp(sg - m)
        total = jnp.sum(pw, axis=1, keepdims=True) + jnp.sum(pg, axis=1, keepdims=True)
        o = (dot(pw.astype(BF), v) + dot(pg.astype(BF), vg)) * (1.0 / total)
        o_ref[rows, :] = apart(o).astype(BF)
        lse_ref[rows, :] = apart(jnp.broadcast_to(m + jnp.log(total), o.shape))


def attend_backward_kernel(
    q_ref, do_ref, k_ref, v_ref, lse_ref, bw_ref, bg_ref,
    dq_ref, dk_ref, dv_ref, dk_acc, dv_acc, *, block, glob_at,
):
    count, window = bw_ref.shape[0], bw_ref.shape[2]
    glob = bg_ref.shape[2]
    dk_acc[...] = jnp.zeros_like(dk_acc)
    dv_acc[...] = jnp.zeros_like(dv_acc)
    at_glob = slice(glob_at, glob_at + glob)
    kg, vg = k_ref[at_glob, :], v_ref[at_glob, :]
    for i in range(count):
        rows = slice(i * block, (i + 1) * block)
        span = slice(i * block, i * block + window)
        k, v = k_ref[span, :], v_ref[span, :]
        qs, dos = both_heads(q_ref[rows, :], 0.125), both_heads(do_ref[rows, :], 1.0)
        lse = jnp.concatenate([lse_ref[rows, h : h + 1] for h in (0, HDIM)], axis=0)
        bw, bg = bw_ref[i], bg_ref[i]
        pw = jnp.exp(dot(qs, k, NT) + jnp.concatenate([bw, bw], axis=0) - lse)
        pg = jnp.exp(dot(qs, kg, NT) + jnp.concatenate([bg, bg], axis=0) - lse)
        tw, tg = dot(dos, v, NT), dot(dos, vg, NT)
        inner = jnp.sum(pw * tw, axis=1, keepdims=True) + jnp.sum(pg * tg, axis=1, keepdims=True)
        dsw, dsg = (pw * (tw - inner)).astype(BF), (pg * (tg - inner)).astype(BF)
        dq_ref[rows, :] = (apart(dot(dsw, k) + dot(dsg, kg)) * 0.125).astype(BF)
        turned_q, turned_do = qs.T, dos.T
        dk_acc[:, span] += dot(turned_q, dsw)
        dk_acc[:, at_glob] += dot(turned_q, dsg)
        dv_acc[:, span] += dot(turned_do, pw.astype(BF))
        dv_acc[:, at_glob] += dot(turned_do, pg.astype(BF))
    for acc, out in ((dk_acc, dk_ref), (dv_acc, dv_ref)):
        for at in range(0, glob_at, 128):
            out[at : at + 128, :] = acc[:, at : at + 128].T.astype(BF)
        out[at_glob, :] = acc[:, at_glob].T.astype(BF)


def by_pair(rows):
    return pl.BlockSpec((rows, PAIR), lambda h: (0, h))


def whole(value):
    return pl.BlockSpec(value.shape, lambda h: (0,) * value.ndim)


def params(mebibytes):
    return pltpu.CompilerParams(vmem_limit_bytes=mebibytes * 1024 * 1024)


SCALAR = pl.BlockSpec(memory_space=pltpu.SMEM)


def once(value):
    return pl.BlockSpec(value.shape, lambda *s: (0,) * value.ndim, pipeline_mode=pl.Buffered(1))


def fixed(shape):
    return pl.BlockSpec(shape, lambda *s: (0,) * len(shape))


def hbm(*values):
    return [pltpu.with_memory_space_constraint(v, pltpu.HBM) if v.ndim > 1 else v for v in values]


def to_hbm(shapes):
    return [pltpu.HBM(v.shape, v.dtype) for v in shapes]


def cost(flops, size):
    return pl.CostEstimate(flops=flops, bytes_accessed=size, transcendentals=0)


def project(at, vecs, xs, pieces, glob, row_n, col_n):
    rows, wide = xs[1].shape
    ext = sum(x.shape[0] for x in xs) + glob
    length, deep = pieces[0].shape
    span = row_n * HDIM
    local = wide // span
    more = glob * col_n
    lane = lambda n: pl.BlockSpec((n, span), lambda i: (0, i))
    shapes = [(rows, wide), (glob, wide), (ext, wide), (ext, wide)]
    outs = [jax.ShapeDtypeStruct(v, BF) for v in shapes]
    outs += [jax.ShapeDtypeStruct((3, glob, wide), F32), jax.ShapeDtypeStruct((glob, wide), BF)]
    last = pl.BlockSpec((more, deep), lambda i: (length // more - 1, 0), pipeline_mode=pl.Buffered(1))
    return pl.pallas_call(
        functools.partial(project_kernel, row_n=row_n, col_n=col_n),
        grid=(local,),
        in_specs=[SCALAR]
        + [once(v) for v in vecs]
        + [once(x) for x in xs]
        + [pl.BlockSpec((3 * HDIM, deep), lambda i: (i, 0)) for _ in pieces]
        + [last for _ in pieces],
        out_specs=[lane(n) for n, _ in shapes]
        + [pl.BlockSpec((3, glob, span), lambda i: (0, 0, i)), fixed((glob, wide))],
        out_shape=to_hbm(outs),
        compiler_params=params(24),
        cost_estimate=cost(6_000_000_000, 10_000_000),
        name="project",
    )(*hbm(at, *vecs, *xs, *pieces, *pieces))


def mlp(o_parts, vecs, col_vecs, at, state, pick, x, cot, weights, row_n, col_n):
    rows, width = x.shape
    deep, hid = width // col_n, weights.shape[2]
    glob = state.shape[1]
    here = lambda i: jnp.where(i < row_n, i, i - row_n)
    back = lambda i: jnp.maximum(i - row_n, 0)
    sds = jax.ShapeDtypeStruct
    outs = [
        sds((rows, width), F32), sds((row_n, col_n, 2, deep, hid), BF), sds((row_n, 8, hid), F32),
        sds((rows, width), F32), sds((rows, width), BF), sds((width, width), BF),
        sds((8, width), F32), sds((glob, width), BF), sds((glob, width), F32),
        sds((glob, width), F32),
    ]
    specs = [fixed(v.shape) for v in outs]
    specs[1] = pl.BlockSpec((1, col_n, 2, deep, hid), lambda i: (back(i), 0, 0, 0, 0))
    specs[2] = pl.BlockSpec((1, 8, hid), lambda i: (back(i), 0, 0))
    count = weights.shape[1] - 2 * deep
    raw = pl.BlockSpec(
        (row_n * col_n, count, hid), lambda i: (0, 2 * deep // count, 0), pipeline_mode=pl.Buffered(1)
    )
    small = [state, pick, x, cot]
    lists = [*o_parts, *vecs, *col_vecs]
    big = [(rows, width)] * 3
    return pl.pallas_call(
        functools.partial(mlp_kernel, row_n=row_n, col_n=col_n, calls=len(o_parts)),
        grid=(2 * row_n,),
        in_specs=[once(v) for v in lists]
        + [SCALAR]
        + [once(v) for v in small]
        + [raw]
        + [pl.BlockSpec((col_n, deep, hid), lambda i, k=k: (here(i), k, 0)) for k in (0, 1)],
        out_specs=specs,
        out_shape=to_hbm(outs),
        scratch_shapes=[
            pltpu.VMEM((8, width), F32),
            pltpu.VMEM((row_n, 8, hid), F32),
            pltpu.VMEM((width, width), BF),
            pltpu.VMEM((rows, width), BF),
            pltpu.VMEM((rows, width), BF),
            pltpu.VMEM((width, rows), BF),
            pltpu.VMEM((row_n, rows, hid), BF),
            pltpu.VMEM((row_n, rows, hid), F32),
            *[pltpu.VMEM(v, F32) for v in big],
            pltpu.VMEM((rows, 128), F32),
            pltpu.VMEM((rows, width), BF),
            pltpu.VMEM((width, rows), BF),
            pltpu.VMEM((rows, hid), F32),
            pltpu.VMEM((rows, hid), BF),
        ],
        compiler_params=params(58),
        cost_estimate=cost(17_000_000_000, 40_000_000),
        name="mlp",
    )(*hbm(*lists, at, *small, weights, weights, weights))


def entry_backward(at, parts, globs, xs, pieces, row_n, col_n, first, shares, gout=None, last=None):
    width = xs[0].shape[1]
    span = row_n * HDIM
    local = width // span
    deep = width // col_n
    ext = sum(x.shape[0] for x in xs)
    lane = lambda v: pl.BlockSpec((v.shape[0], shares * span), lambda i: (0, first // shares))
    piece = pl.BlockSpec((3 * shares * HDIM, deep), lambda i: (first // shares, 0))
    qg, dog, k_ext, v_ext, lse, og, keep = globs
    args = [p[j] for j in range(3) for p in parts]
    specs = [SCALAR] + [once(v) for v in args]
    args += globs
    specs += [lane(v) for v in globs[:-1]] + [once(keep)]
    args += xs
    specs += [once(v) for v in xs]
    args += pieces
    specs += [piece for _ in pieces]
    rest = list(last) if last else [gout]
    args += rest
    specs += [once(v) for v in rest]
    length, more = 3 * shares * HDIM, None
    if last:
        lines = last[2].shape[2] // deep + 6 + 2 * local
        more = (-(-lines // 32) * 32, 2 * (local - shares))
        length += more[0]
    else:
        length += width // row_n
    shape = jax.ShapeDtypeStruct((row_n // 2, length, width), BF)
    outs = [shape, shape, jax.ShapeDtypeStruct((ext, width), F32)]
    if not last:
        outs.append(jax.ShapeDtypeStruct((8, span), F32))
    return pl.pallas_call(
        functools.partial(
            entry_backward_kernel, row_n=row_n, col_n=col_n, calls=len(parts), shares=shares,
            last=last is not None, more=more,
        ),
        grid=(1,),
        in_specs=specs,
        out_specs=[fixed(v.shape) for v in outs],
        out_shape=to_hbm(outs),
        compiler_params=params(48),
        cost_estimate=cost(3_000_000_000 * shares, 8_000_000 * shares),
        name="entry_backward",
    )(*hbm(at, *args))


def some_pairs(rows, first):
    return pl.BlockSpec((rows, PAIR), lambda h: (0, h + first))


def attend_forward(q, k_ext, v_ext, bias_w, bias_g, glob_at, first, count):
    rows = q.shape[0]
    ext = k_ext.shape[0]
    block = bias_w.shape[1]
    wide = count * PAIR
    return pl.pallas_call(
        functools.partial(attend_forward_kernel, block=block, glob_at=glob_at),
        grid=(count,),
        in_specs=[some_pairs(rows, first), some_pairs(ext, first), some_pairs(ext, first)]
        + [whole(bias_w), whole(bias_g)],
        out_specs=[by_pair(rows), by_pair(rows)],
        out_shape=to_hbm(
            [jax.ShapeDtypeStruct((rows, wide), BF), jax.ShapeDtypeStruct((rows, wide), F32)]
        ),
        compiler_params=params(20),
        cost_estimate=pl.CostEstimate(
            flops=3_500_000_000, bytes_accessed=4_000_000, transcendentals=1_700_000
        ),
        name="attend_forward",
    )(*hbm(q, k_ext, v_ext, bias_w, bias_g))


def attend_backward(q, do, k_ext, v_ext, lse, bias_w, bias_g, glob_at, first, count, inside):
    rows = q.shape[0]
    ext = k_ext.shape[0]
    block = bias_w.shape[1]
    wide = count * PAIR
    return pl.pallas_call(
        functools.partial(attend_backward_kernel, block=block, glob_at=glob_at),
        grid=(count,),
        in_specs=[some_pairs(rows, first), some_pairs(rows, first)]
        + [some_pairs(ext, first), some_pairs(ext, first), some_pairs(rows, inside)]
        + [whole(bias_w), whole(bias_g)],
        out_specs=[by_pair(rows), by_pair(ext), by_pair(ext)],
        out_shape=to_hbm(
            [
                jax.ShapeDtypeStruct((rows, wide), BF),
                jax.ShapeDtypeStruct((ext, wide), BF),
                jax.ShapeDtypeStruct((ext, wide), BF),
            ]
        ),
        scratch_shapes=[pltpu.VMEM((PAIR, ext), F32), pltpu.VMEM((PAIR, ext), F32)],
        compiler_params=params(24),
        cost_estimate=pl.CostEstimate(
            flops=8_000_000_000, bytes_accessed=5_000_000, transcendentals=1_700_000
        ),
        name="attend_backward",
    )(*hbm(q, do, k_ext, v_ext, lse, bias_w, bias_g))


def norm_forward(resid, gain, shift_by):
    center = jnp.mean(resid, axis=1, keepdims=True)
    apart = resid - center
    scale = lax.rsqrt(jnp.mean(apart * apart, axis=1, keepdims=True) + 1e-05)
    normed = apart * scale
    return normed * gain + shift_by, normed, scale


def norm_backward(grad, normed, scale, gain):
    scaled = grad * gain
    total = jnp.mean(scaled, axis=1, keepdims=True)
    mixed = jnp.mean(scaled * normed, axis=1, keepdims=True)
    return scale * (scaled - total - normed * mixed)


def on_device(
    hidden_in, w_query, b_query, w_key, w_value, b_value, w_out, b_out, gain_attn, bias_attn,
    w_in, b_in, w_ffout, b_ffout, gain_ffn, bias_ffn, glob_pos, cotangent,
):
    row_n, col_n = lax.axis_size("row"), lax.axis_size("col")
    row_i, col_i = lax.axis_index("row"), lax.axis_index("col")
    rows = hidden_in.shape[0]
    wide, deep = w_query.shape[1], w_query.shape[0]
    hid = w_in.shape[1]
    local = wide // HDIM
    glob_row = glob_pos[0]
    glob = glob_row.shape[0]
    me = row_i * col_n + col_i
    halo = Halo(rows, row_n * col_n)
    is_prompt = me < halo.half

    own_rows = me * rows + jnp.arange(rows, dtype=jnp.int32)
    flags = [row_i, col_i, is_prompt.astype(jnp.int32), me * rows]
    at = jnp.stack([jnp.asarray(v, jnp.int32) for v in flags])
    message = pack(at, glob_row[None], hidden_in, w_query.T, w_key.T, w_value.T, col_n)
    vectors = (b_query, b_value, b_in, b_out, gain_attn, bias_attn, b_ffout, gain_ffn, bias_ffn)
    message, x_sent, vectors, w_in, w_out, w_ffout = fence(
        message, hidden_in, vectors, w_in, w_out, w_ffout
    )
    b_query, b_value, b_in, b_out, gain_attn, bias_attn, b_ffout, gain_ffn, bias_ffn = vectors
    pieces = gather_far(message)
    x_left, x_right, hop = halo.fetch(x_sent, is_prompt)
    ratio = hid // deep
    both = jnp.concatenate(
        [w_in, w_ffout, jnp.concatenate(jnp.split(w_out, ratio, axis=0), axis=1)], axis=0
    ).astype(BF)
    vec_row = jnp.pad(b_query.reshape(local, HDIM), ((0, 16 - local), (0, 128 - HDIM)))
    vec_row += jnp.pad(b_value.reshape(local, HDIM), ((0, 16 - local), (HDIM, 128 - 2 * HDIM)))
    vec_row += jnp.pad(b_in.reshape(-1, 128), ((local, 16 - local - hid // 128), (0, 0)))
    vec_col = jnp.zeros((8, deep), F32)
    for i, v in enumerate((b_out, gain_attn, bias_attn, b_ffout, gain_ffn, bias_ffn)):
        vec_col += jnp.pad(v[None], ((i, 7 - i), (0, 0)))
    hop, vec_row, vec_col, both = fence(hop, vec_row, vec_col, both)
    weights = lax.all_gather(both, ("row", "col"), axis=0)
    row_vec, col_vec = {0: vec_row}, {0: vec_col}
    for bit in (1 << i for i in range((row_n - 1).bit_length())):
        row_vec.update({a ^ bit: swap(v, ("row", bit)) for a, v in list(row_vec.items())})
    for bit in (1 << i for i in range((col_n - 1).bit_length())):
        col_vec.update({b ^ bit: swap(v, ("col", bit)) for b, v in list(col_vec.items())})
    vecs = [row_vec[a] for a in range(row_n)]
    col_vecs = [col_vec[b] for b in range(col_n)]

    pieces = gather_near(pieces)
    names = [(a, b) for a in range(row_n) for b in range(col_n)]
    pick = (own_rows[:, None] == glob_row[None, :]).astype(BF)

    own_at, glob_at = WIN, 2 * WIN + rows
    block = min(rows, WIN)
    bias_w, bias_g = bias_blocks(own_rows, halo.key_rows(me, is_prompt), glob_row, block)
    keep = jnp.where(is_prompt, 0.0, NEG) * jnp.ones((1, rows), F32)
    piece_list = [pieces[k] for k in names]
    q, qg, k_ext, v_ext, state, x_glob = project(
        at, vecs, [x_left, hidden_in, x_right], piece_list, glob, row_n, col_n
    )
    xs = [x_left, hidden_in, x_right, x_glob]

    span = row_n * HDIM
    share = span // PAIR
    rounds = [step for step in far_steps() if step != ("row", row_n // 2)] + [NEAR]
    rounds = [rounds[:-1], rounds[-1:]]
    calls = [(0, (local - 1) * share), ((local - 1) * share, share)]
    o_parts, lse_parts = [], []
    for i, (first_pair, count) in enumerate(calls):
        o_part, lse_part = attend_forward(
            q, k_ext, v_ext, bias_w, bias_g, glob_at, first_pair, count
        )
        o_parts.append(o_part)
        lse_parts.append(lse_part)
        for step in rounds[i]:
            state = merge_states(state, swap(state, step), step)
        if i == 0:
            state, q, o_parts[-1] = fence(state, q, o_part)

    hidden_out, grads, grad_b_in, d_resid1, d_o, out_grads, sums, dog, og, lse_g = mlp(
        o_parts, vecs, col_vecs, at, state, pick, hidden_in, cotangent, weights, row_n, col_n
    )
    grads = grads.reshape(row_n * col_n, 2 * deep, hid)
    grads = lax.psum_scatter(grads, ("row", "col"), scatter_dimension=0, tiled=True)[0]

    def attend_share(i, d_o):
        at_call = min(i // (local - 1), 1)
        inside = i * share - calls[at_call][0]
        return attend_backward(
            q, d_o, k_ext, v_ext, lse_parts[at_call], bias_w, bias_g, glob_at, i * share, share, inside
        )

    parts = []
    for i in range(local - 1):
        parts.append(attend_share(i, d_o))
        for step in rounds[i] if i < len(rounds) else []:
            dog = add_heads(dog, swap(dog, step), step)
        if i < local - 2:
            dog, d_o, parts[-1] = fence(dog, d_o, parts[-1])
    globs = [qg, dog, k_ext, v_ext, lse_g, og, keep]
    keep_rows, send_rows, dx, totals = entry_backward(
        at, parts, globs, xs, piece_list, row_n, col_n, 0, local - 1, gout=out_grads
    )
    near = near_pieces(at, keep_rows, swap(send_rows, NEAR), col_n)
    near, d_o = fence(near, d_o)
    part = attend_share(local - 1, d_o)
    keep_rows, send_rows, dx = entry_backward(
        at, [part], globs, xs, piece_list, row_n, col_n, local - 1, 1,
        last=(dx, totals, grad_b_in, sums),
    )
    own_first = seq_scatter(far_sum(near))
    got, grads, own_first = fence(swap(send_rows, NEAR), grads, own_first)
    grads = lax.psum(grads, "seq")
    near = near_pieces(at, keep_rows, got, col_n)
    near, dx = fence(near, dx)
    own_last = seq_scatter(far_sum(near))
    split = own_first.shape[0]
    both = seq_gather(jnp.concatenate([own_first, own_last], axis=0))
    entry_first = jnp.concatenate([v[:split] for v in both], axis=0).astype(F32)
    entry_last = jnp.concatenate([v[split:] for v in both], axis=0).astype(F32)
    _, grads = fence(entry_last, grads)
    grads = grads.astype(F32)

    dx_glob = group_sum(dx[glob_at:], lambda a, b, step: a + b)
    first, last = halo.give(dx[:WIN], dx[own_at + rows : glob_at], is_prompt)
    grad_x = d_resid1 + dx[own_at : own_at + rows]
    grad_x = grad_x + lax.dot_general(
        pick.astype(F32), dx_glob, NN, precision=lax.Precision.HIGHEST, preferred_element_type=F32
    )
    size = first.shape[0]
    grad_x = jnp.concatenate([grad_x[:size] + first, grad_x[size:]], axis=0)
    grad_x = jnp.concatenate([grad_x[:-size], grad_x[-size:] + last], axis=0)

    cut = 3 * (local - 1) * HDIM
    by_kind = jnp.concatenate([entry_first[:cut], entry_last[: 3 * HDIM]], axis=0)
    by_kind = by_kind.reshape(local, 3, HDIM, deep)
    grad_out = entry_first[cut:]
    tail = entry_last[3 * HDIM :]
    b_rows = hid // deep
    bias_rows = tail[b_rows + 6 : b_rows + 6 + 2 * local, :HDIM].reshape(local, 2, HDIM)
    col_vectors = tail[b_rows : b_rows + 6]
    return (
        hidden_out,
        grad_x,
        by_kind[:, 0].reshape(wide, deep).T,
        bias_rows[:, 0].reshape(wide),
        by_kind[:, 1].reshape(wide, deep).T,
        by_kind[:, 2].reshape(wide, deep).T,
        bias_rows[:, 1].reshape(wide),
        grad_out,
        col_vectors[0],
        col_vectors[1],
        col_vectors[2],
        grads[deep:],
        tail[:b_rows].reshape(-1),
        grads[:deep],
        col_vectors[3],
        col_vectors[4],
        col_vectors[5],
    )


def solution(mesh):
    tokens = P(("seq", "row", "col"), None)
    both, row, col = P("col", "row"), P("row"), P("col")
    in_specs = (
        tokens, both, row, both, both, row, P("row", "col"), col, col, col, both, row, both, col,
        col, col, P("seq", None), tokens,
    )
    out_specs = (
        tokens, tokens, both, row, both, both, row, P("row", "col"), col, col, col, both, row,
        both, col, col, col,
    )
    return jax.shard_map(
        on_device, mesh=mesh, in_specs=in_specs, out_specs=out_specs, check_vma=False
    )
```

```python
import functools
import math

import jax
import jax.numpy as jnp
from jax import lax
from jax.experimental import pallas as pl
from jax.experimental.pallas import tpu as pltpu
from jax.sharding import PartitionSpec as P

D = 768
HDIM = 64
WIN = 256
PLEN = 2048
LC = 256
PAIR = 2 * HDIM
FAR = -(1 << 20)
BF = jnp.bfloat16
F32 = jnp.float32
NEG = -1e30

NN = (((1,), (0,)), ((), ()))
NT = (((1,), (1,)), ((), ()))
TN = (((0,), (0,)), ((), ()))


def dot(a, b, dims=NN):
    return lax.dot_general(a, b, dims, preferred_element_type=F32)


def swap(value, step):
    axis, bit = step
    size = lax.axis_size(axis)
    return lax.ppermute(value, axis, [(i, i ^ bit) for i in range(size)])


def far_steps():
    rows, cols = lax.axis_size("row"), lax.axis_size("col")
    steps, bit = [], 1
    while bit < cols:
        steps.append(("col", bit))
        bit *= 2
    bit = 2
    while bit < rows:
        steps.append(("row", bit))
        bit *= 2
    return steps


NEAR = ("row", 1)


def move(name, step):
    axis, bit = step
    return (name[0] ^ bit, name[1]) if axis == "row" else (name[0], name[1] ^ bit)


def fence(*values):
    return lax.optimization_barrier(values)


def swap_both(value, row_bit, col_bit):
    rows, cols = lax.axis_size("row"), lax.axis_size("col")
    pairs = [
        (r * cols + c, (r ^ row_bit) * cols + (c ^ col_bit))
        for r in range(rows)
        for c in range(cols)
    ]
    return lax.ppermute(value, ("row", "col"), pairs)


def far_names():
    rows, cols = lax.axis_size("row"), lax.axis_size("col")
    return [(a, b) for a in range(0, rows, 2) for b in range(cols) if (a, b) != (0, 0)]


def gather_far(own):
    far = far_steps()
    pieces = {(0, 0): own}
    if len(far) != 2:
        return pieces | {name: swap_both(own, *name) for name in far_names()}
    first, second = far
    a, b = swap(own, first), swap(own, second)
    half = own.shape[0] // 2
    corner = [swap(b[:half], first), swap(a[half:], second)]
    at_first, at_second = move((0, 0), first), move((0, 0), second)
    return pieces | {
        at_first: a,
        at_second: b,
        move(at_first, second): jnp.concatenate(corner, axis=0),
    }


def gather_near(pieces):
    return pieces | {move(k, NEAR): swap(v, NEAR) for k, v in pieces.items()}


def in_order(parts, me):
    bit = 1
    while bit < len(parts):
        odd = (me & bit) != 0
        parts = [jnp.where(odd, parts[t ^ bit], parts[t]) for t in range(len(parts))]
        bit *= 2
    return parts


def near_kernel(at_ref, keep_ref, got_ref, *out_refs, col_n):
    for half in range(keep_ref.shape[0]):
        near = keep_ref[half].astype(F32) + got_ref[half].astype(F32)
        for b, part in enumerate(columns(near, col_n, at_ref[1])):
            out = out_refs[half * col_n + b]
            out[...] = part.astype(out.dtype)


def near_pieces(at, keep, got, col_n):
    halves, length, width = keep.shape
    count = halves * col_n
    piece = (length, width // col_n)
    shapes = [jax.ShapeDtypeStruct(piece, BF if i else F32) for i in range(count)]
    return pl.pallas_call(
        functools.partial(near_kernel, col_n=col_n),
        in_specs=[SCALAR] + [pl.BlockSpec(memory_space=pltpu.VMEM)] * 2,
        out_shape=to_hbm(shapes),
        compiler_params=params(24),
        name="near_pieces",
    )(*hbm(at, keep, got))


def far_sum(parts):
    cols = lax.axis_size("col")
    total = parts[0]
    far = far_steps()
    if len(far) == 2:
        first, second = far
        _, one, two, corner = parts
        half = corner.shape[0] // 2
        low = two[:half].astype(F32) + swap(corner[:half], first).astype(F32)
        high = one[half:].astype(F32) + swap(corner[half:], second).astype(F32)
        one = jnp.concatenate([one[:half], high.astype(BF)], axis=0)
        two = jnp.concatenate([low.astype(BF), two[half:]], axis=0)
        return total + swap(one, first).astype(F32) + swap(two, second).astype(F32)
    for a, b in far_names():
        total = total + swap_both(parts[a // 2 * cols + b], a, b).astype(F32)
    return total


def seq_turn(part, k):
    count = lax.axis_size("seq")
    return lax.ppermute(part, "seq", [(i, (i + k) % count) for i in range(count)])


def seq_scatter(value):
    count, me = lax.axis_size("seq"), lax.axis_index("seq")
    parts = value.astype(BF).reshape((count, value.shape[0] // count) + value.shape[1:])
    total = lax.dynamic_index_in_dim(parts, me, 0, keepdims=False).astype(F32)
    for k in range(1, count):
        part = lax.dynamic_index_in_dim(parts, (me + k) % count, 0, keepdims=False)
        total = total + seq_turn(part, k).astype(F32)
    return total.astype(BF)


def seq_gather(own):
    count, me = lax.axis_size("seq"), lax.axis_index("seq")
    held = jnp.stack([own] + [seq_turn(own, k) for k in range(1, count)])
    return [lax.dynamic_index_in_dim(held, (me - i) % count, 0, keepdims=False) for i in range(count)]


def group_sum(value, merge):
    for step in far_steps() + [NEAR]:
        value = merge(value, swap(value, step), step)
    return value


def shift(value, pairs):
    return lax.ppermute(value, ("row", "col"), pairs) if pairs else jnp.zeros_like(value)


class Halo:
    def __init__(self, rows, devices):
        self.rows = rows
        self.n = devices
        self.half = PLEN // rows
        self.block = min(rows, WIN)
        self.steps = WIN // self.block
        self.wide = rows >= 2 * WIN

    def pairs_left(self, t):
        return [(j - t, j) for j in range(self.half) if j >= t]

    def pairs_right(self, t):
        return [(j + t, j) for j in range(self.half) if j + t < self.half]

    def pairs_mates(self, t):
        return [(self.mate(j, t), j) for j in range(self.half, self.n)]

    def mate(self, j, t):
        base = j - j % self.steps
        return base + (j - base + t) % self.steps

    def tree(self, t):
        source = self.half - self.steps + t
        rounds, bit = [[(source, source + self.half)]], 1
        have = [source + self.half]
        while len(have) < self.n - self.half:
            rounds.append([(d, d ^ bit) for d in have])
            have += [d ^ bit for d in have]
            bit *= 2
        return rounds

    def fetch(self, own, is_prompt):
        first, last = own[: self.block], own[-self.block :]
        left, right, tail = [], [], []
        for t in range(self.steps, 0, -1):
            at = self.steps - t
            rounds = self.tree(at)
            if self.steps == 1:
                left.append(shift(last, self.pairs_left(t) + rounds[0]))
                mixed = jnp.where(is_prompt, first, left[0])
                right.append(shift(mixed, self.pairs_right(t) + rounds[1]))
                held = left[0] + jnp.where(is_prompt, jnp.zeros((), BF), right[0])
                rounds = rounds[2:]
            else:
                left.append(shift(last, self.pairs_left(t)))
                right.append(shift(first, self.pairs_right(at + 1)))
                held = shift(last, rounds[0])
                rounds = rounds[1:]
            for pairs in rounds:
                held = held + shift(held, pairs)
            tail.append(held)
        hop = left[0]
        left = [jnp.where(is_prompt, a, b) for a, b in zip(left, tail)]
        if self.wide:
            right = [jnp.where(is_prompt, a, b) for a, b in zip(right, tail)]
        elif self.steps > 1:
            mates = [shift(own, self.pairs_mates(t)) for t in range(1, self.steps)]
            right = [jnp.where(is_prompt, a, b) for a, b in zip(right, mates)] + right[len(mates) :]
        return jnp.concatenate(left, axis=0), jnp.concatenate(right, axis=0), hop

    def give(self, left, right, is_prompt):
        block = self.block

        def cut(value):
            return [value[t * block : (t + 1) * block] for t in range(self.steps)]

        def back(value, pairs):
            return shift(value, [(b, a) for a, b in pairs]).astype(F32)

        zero = jnp.zeros((), F32)
        left, right = cut(left), cut(right)
        first = jnp.zeros((block, left[0].shape[1]), F32)
        last = first
        for i, t in enumerate(range(self.steps, 0, -1)):
            last = last + back(left[i].astype(BF), self.pairs_left(t))
        for i, t in enumerate(range(1, self.steps + 1)):
            first = first + back(right[i].astype(BF), self.pairs_right(t))
        for t in range(self.steps):
            held = left[t] + right[t] if self.wide else left[t]
            held = jnp.where(is_prompt, zero, held)
            rounds = self.tree(t)
            for pairs in reversed(rounds[1:]):
                held = held + back(held.astype(BF), pairs)
            last = last + back(held.astype(BF), rounds[0])
        if not self.wide:
            for t in range(1, self.steps):
                first = first + back(right[t - 1].astype(BF), self.pairs_mates(t))
        return first, last

    def key_rows(self, me, is_prompt):
        near = jnp.arange(WIN, dtype=jnp.int32)
        start = me * self.rows
        left = start - WIN + near
        left = jnp.where(left < 0, FAR, left)
        left = jnp.where(is_prompt, left, PLEN - WIN + near)
        right = start + self.rows + near
        right = jnp.where(right < PLEN, right, FAR)
        if self.wide:
            other = PLEN - WIN + near
        elif self.steps > 1:
            parts = [
                (me - me % self.steps + (me % self.steps + t) % self.steps) * self.rows
                + jnp.arange(self.rows, dtype=jnp.int32)
                for t in range(1, self.steps)
            ]
            other = jnp.concatenate(parts + [jnp.full((self.rows,), FAR, jnp.int32)])
        else:
            other = jnp.full((WIN,), FAR, jnp.int32)
        right = jnp.where(is_prompt, right, other)
        own = start + jnp.arange(self.rows, dtype=jnp.int32)
        return jnp.concatenate([left, own, right])


def place_of(index):
    after = index - PLEN
    return jnp.where(index < PLEN, index, PLEN + after % LC)


def bias_blocks(query_rows, key_rows, glob_row, block):
    count = query_rows.shape[0] // block
    query = query_rows.reshape(count, block, 1)
    keys = jnp.stack([key_rows[i * block : i * block + 2 * WIN + block] for i in range(count)])
    keys = keys[:, None, :]
    near = (jnp.abs(place_of(query) - keys) <= WIN) & (keys < PLEN) & (keys >= 0)
    same = (query >= PLEN) & (keys >= PLEN) & ((query - PLEN) // LC == (keys - PLEN) // LC)
    window = jnp.where(near | same, 0.0, NEG).astype(F32)
    beyond = jnp.abs(place_of(query) - glob_row[None, None, :]) > WIN
    return window, jnp.where(beyond, 0.0, NEG).astype(F32)


def lanes(shape):
    return lax.broadcasted_iota(jnp.int32, shape, 1) < HDIM


def one_head(value, half, scale):
    keep = lanes(value.shape)
    keep = keep if half == 0 else ~keep
    return (jnp.where(keep, value.astype(F32), 0.0) * scale).astype(BF)


def stacked(value, scale):
    head = lax.broadcasted_iota(jnp.int32, value.shape, 1) // HDIM
    value = value.astype(F32) * scale
    parts = [jnp.where(head == h, value, 0.0) for h in range(value.shape[1] // HDIM)]
    return jnp.concatenate(parts, axis=0)


def unstacked(value, count):
    shape = (count, value.shape[1])
    head = lax.broadcasted_iota(jnp.int32, shape, 1) // HDIM
    out = jnp.zeros(shape, F32)
    for h in range(value.shape[0] // count):
        out = jnp.where(head == h, value[h * count : (h + 1) * count, :], out)
    return out


def glob_state(q, k, v, keep):
    count, wide = q.shape
    s = dot(stacked(q, 0.125).astype(BF), k, NT) + keep
    m = jnp.max(s, axis=1, keepdims=True)
    p = jnp.exp(s - m)
    total = jnp.sum(p, axis=1, keepdims=True)
    o = dot(p.astype(BF), v)
    return [unstacked(jnp.broadcast_to(t, o.shape), count) for t in (o, m, total)]


def share_rows(refs, share, kind):
    at = (share * 3 + kind) * HDIM
    return jnp.concatenate([r[at : at + HDIM, :] for r in refs], axis=0)


def columns(value, count, me):
    size = value.shape[1] // count
    return in_order([value[:, c * size : (c + 1) * size] for c in range(count)], me)


def pack_kernel(at_ref, glob_ref, x_ref, wq_ref, wk_ref, wv_ref, out_ref, *, col_n, glob_at):
    rows, width = x_ref.shape
    deep, local = width // col_n, wq_ref.shape[0] // HDIM
    for kind, w_ref in enumerate((wq_ref, wk_ref, wv_ref)):
        for i in range(local):
            at = (i * 3 + kind) * HDIM
            out_ref[at : at + HDIM, :] = w_ref[i * HDIM : (i + 1) * HDIM, :].astype(BF)
    glob = glob_ref.shape[1]
    row = lax.broadcasted_iota(jnp.int32, (rows, glob), 0) + at_ref[3]
    pick = (row == glob_ref[...]).astype(F32).astype(BF)
    own = dot(pick, x_ref[...], TN).astype(BF)
    for c in range(col_n):
        at = glob_at + c * glob
        out_ref[at : at + glob, :] = own[:, c * deep : (c + 1) * deep]


def pack(at, glob_row, x, w_query, w_key, w_value, col_n):
    wide, deep = w_query.shape
    more = glob_row.shape[1] * col_n
    glob_at = -(-3 * wide // more) * more
    return pl.pallas_call(
        functools.partial(pack_kernel, col_n=col_n, glob_at=glob_at),
        in_specs=[SCALAR] + [pl.BlockSpec(memory_space=pltpu.VMEM)] * 5,
        out_shape=pltpu.HBM((glob_at + more, deep), BF),
        compiler_params=params(16),
        name="pack",
    )(*hbm(at, glob_row, x, w_query, w_key, w_value))


def project_kernel(at_ref, *refs, row_n, col_n):
    vecs, refs = refs[:row_n], refs[row_n:]
    (left_ref, own_ref, right_ref), refs = refs[:3], refs[3:]
    pieces, refs = refs[: row_n * col_n], refs[row_n * col_n :]
    extra, refs = refs[: row_n * col_n], refs[row_n * col_n :]
    q_ref, qg_ref, k_ref, v_ref, state_ref, xg_ref = refs
    share, col = pl.program_id(0), at_ref[1]
    span = row_n * HDIM
    glob = xg_ref.shape[0]
    total = functools.reduce(jnp.add, [r[...].astype(F32) for r in extra])
    parts = [total[c * glob : (c + 1) * glob, :] for c in range(col_n)]
    xg = jnp.concatenate(parts, axis=1).astype(BF)
    xg_ref[...] = xg
    lines = [r[pl.ds(share, 1), :] for r in vecs]
    bias_q = jnp.concatenate([v[:, :HDIM] for v in lines], axis=1)
    bias_v = jnp.concatenate([v[:, HDIM : 2 * HDIM] for v in lines], axis=1)
    mats = []
    for b in range(col_n):
        refs_b = [pieces[a * col_n + b] for a in range(row_n)]
        mats.append(jnp.concatenate([share_rows(refs_b, 0, kind) for kind in range(3)], axis=0))

    at = 0
    for g, x in enumerate((left_ref[...], own_ref[...], right_ref[...], xg)):
        rows = slice(at, at + x.shape[0])
        at += x.shape[0]
        first = 0 if g in (1, 3) else span
        total = 0.0
        for part, mat in zip(columns(x, col_n, col), mats):
            total = total + dot(part, mat[first:, :], NT)
        k_ref[rows, :] = total[:, span - first : 2 * span - first].astype(BF)
        v_ref[rows, :] = (total[:, 2 * span - first :] + bias_v).astype(BF)
        if first == 0:
            out = q_ref if g == 1 else qg_ref
            out[...] = (total[:, :span] + bias_q).astype(BF)
    rows = slice(left_ref.shape[0], left_ref.shape[0] + own_ref.shape[0])
    keep = jnp.where(at_ref[2] > 0, 0.0, NEG)
    state = glob_state(qg_ref[...], k_ref[rows, :], v_ref[rows, :], keep)
    for i in range(3):
        state_ref[i] = state[i]


def swap_heads(value, bit):
    blocks = [value[..., i * PAIR : (i + 1) * PAIR] for i in range(value.shape[-1] // PAIR)]
    if bit == 1:
        return [pltpu.roll(v, HDIM, v.ndim - 1) for v in blocks]
    return [blocks[i ^ (bit // 2)] for i in range(len(blocks))]


def merged(one_ref, two_ref, bit):
    for i in range(one_ref.shape[2] // PAIR):
        span = slice(i * PAIR, (i + 1) * PAIR)
        o1, m1, l1 = [one_ref[j, :, span] for j in range(3)]
        o2, m2, l2 = [swap_heads(two_ref[j], bit)[i] for j in range(3)]
        top = jnp.maximum(m1, m2)
        a, b = jnp.exp(m1 - top), jnp.exp(m2 - top)
        yield span, (o1 * a + o2 * b, top, l1 * a + l2 * b)


def merge_kernel(one_ref, two_ref, out_ref, *, bit):
    for span, terms in merged(one_ref, two_ref, bit):
        for j, term in enumerate(terms):
            out_ref[j, :, span] = term


def add_heads_kernel(one_ref, two_ref, out_ref, *, bit):
    for i, block in enumerate(swap_heads(two_ref[...].astype(F32), bit)):
        span = slice(i * PAIR, (i + 1) * PAIR)
        out_ref[:, span] = (one_ref[:, span].astype(F32) + block).astype(BF)


def head_bit(step):
    return step[1] if step[0] == "row" else 0


def merge_states(one, two, step):
    return pl.pallas_call(
        functools.partial(merge_kernel, bit=head_bit(step)),
        out_shape=jax.ShapeDtypeStruct(one.shape, one.dtype),
        name="merge_states",
    )(one, two)


def add_heads(one, two, step):
    return pl.pallas_call(
        functools.partial(add_heads_kernel, bit=head_bit(step)),
        out_shape=jax.ShapeDtypeStruct(one.shape, one.dtype),
        name="add_heads",
    )(one, two)


def chunks(rows):
    size = min(rows, 128)
    return [slice(i, i + size) for i in range(0, rows, size)]


def gelu_parts(u):
    density = jnp.exp(u * u * -0.5)
    t = 1.0 / (1.0 + 0.2316418863 * jnp.abs(u))
    poly = 1.061405429 * t - 1.453152027
    poly = poly * t + 1.421413741
    poly = poly * t - 0.284496736
    poly = poly * t + 0.254829592
    tail = 0.5 * poly * t * density
    phi = jnp.where(u >= 0.0, 1.0 - tail, tail)
    return u * phi, phi + u * density * 0.3989422804014327


def column_sum(value):
    return jnp.sum(value, axis=0, keepdims=True)


def mlp_kernel(*refs, row_n, col_n, calls, bit):
    o_parts, refs = refs[:calls], refs[calls:]
    vecs, refs = refs[:row_n], refs[row_n:]
    col_vecs, refs = refs[:col_n], refs[col_n:]
    (
        at_ref, state_ref, other_ref, pick_ref, x_ref, cot_ref, wraw_ref, win_ref, wff_ref,
        out_ref, grads_ref, gbin_ref, dres_ref, do_ref, gout_ref, sums_ref, dog_ref, og_ref, lse_ref,
        vec_ref, bin_ref, wo_ref, o_ref, low_ref, lowt_ref, act_ref, slope_ref, f_ref, hid_ref,
        normed_ref, scale_ref, df_ref, dft_ref, u_ref, du_ref,
    ) = refs
    step = pl.program_id(0)
    rows, width = x_ref.shape
    deep, local, hid = width // col_n, width // (row_n * HDIM), win_ref.shape[2]

    @pl.when(step == 0)
    def _():
        parts = in_order([v[...] for v in col_vecs], at_ref[1])
        vec_ref[...] = jnp.concatenate(parts, axis=1)
        for r, part in enumerate(in_order([v[...] for v in vecs], at_ref[0])):
            lines = [part[local + j : local + j + 1, :] for j in range(hid // 128)]
            bin_ref[r] = jnp.broadcast_to(jnp.concatenate(lines, axis=1), bin_ref.shape[1:])
        count = wraw_ref.shape[1]
        unit = math.gcd(HDIM, count)
        for a in range(row_n):
            for c in range(col_n):
                raw = wraw_ref[jnp.bitwise_xor(at_ref[0], a) * col_n + c]
                for row in range(0, local * HDIM, unit):
                    to = (row // HDIM * row_n + a) * HDIM + row % HDIM
                    part, off = row // count, row % count
                    wo_ref[to : to + unit, c * deep : (c + 1) * deep] = raw[
                        off : off + unit, part * deep : (part + 1) * deep
                    ]
        for span, (out, top, total) in merged(state_ref, other_ref, bit):
            og_ref[:, span] = out / total
            lse_ref[:, span] = top + jnp.log(total)
        og = og_ref[...].astype(BF)
        for cut in chunks(rows):
            pick = pick_ref[cut, :]
            is_glob = jnp.sum(pick.astype(F32), axis=1, keepdims=True) > 0.5
            o = jnp.concatenate([r[cut, :] for r in o_parts], axis=1)
            o_ref[cut, :] = jnp.where(is_glob, dot(pick, og), o.astype(F32)).astype(BF)
        f_ref[...] = dot(o_ref[...], wo_ref[...])
        for cut in chunks(rows):
            resid = x_ref[cut, :].astype(F32) + f_ref[cut, :] + vec_ref[0:1, :]
            hidden, normed, scale = norm_forward(resid, vec_ref[1:2, :], vec_ref[2:3, :])
            hid_ref[cut, :] = hidden
            low = hidden.astype(BF)
            low_ref[cut, :] = low
            lowt_ref[:, cut] = low.T
            normed_ref[cut, :] = normed
            scale_ref[cut, :] = jnp.broadcast_to(scale, (scale.shape[0], scale_ref.shape[1]))
        f_ref[...] = jnp.zeros_like(f_ref)

    @pl.when(step < row_n)
    def _():
        u_ref[...] = dot(low_ref[...], win_ref[...].reshape(width, -1))
        for cut in chunks(rows):
            act, slope = gelu_parts(u_ref[cut, :] + bin_ref[step, 0:1, :])
            act_ref[step, cut, :] = act.astype(BF)
            slope_ref[step, cut, :] = slope
        f_ref[...] += dot(act_ref[step], wff_ref[...].reshape(width, -1), NT)

    @pl.when(step == row_n - 1)
    def _():
        gain, bias, low = 0.0, 0.0, 0.0
        for cut in chunks(rows):
            resid = hid_ref[cut, :] + f_ref[cut, :] + vec_ref[3:4, :]
            out, normed, scale = norm_forward(resid, vec_ref[4:5, :], vec_ref[5:6, :])
            out_ref[cut, :] = out
            g = cot_ref[cut, :].astype(F32)
            d = norm_backward(g, normed, scale, vec_ref[4:5, :])
            f_ref[cut, :] = d
            d_low = d.astype(BF)
            df_ref[cut, :] = d_low
            dft_ref[:, cut] = d_low.T
            gain = gain + column_sum(g * normed)
            bias = bias + column_sum(g)
            low = low + column_sum(d_low.astype(F32))
        sums_ref[3:4, :] = low
        sums_ref[4:5, :] = gain
        sums_ref[5:6, :] = bias
        sums_ref[6:8, :] = jnp.zeros((2, width), F32)

    @pl.when(step >= row_n)
    def _():
        now = step - row_n
        u_ref[...] = dot(df_ref[...], wff_ref[...].reshape(width, -1))
        grad = dot(dft_ref[...], act_ref[now]).astype(BF)
        grads_ref[0, :, 0] = grad.reshape(col_n, deep, -1)
        total = 0.0
        for cut in chunks(rows):
            d_u = (u_ref[cut, :] * slope_ref[now, cut, :]).astype(BF)
            du_ref[cut, :] = d_u
            total = total + column_sum(d_u.astype(F32))
        gbin_ref[0] = jnp.broadcast_to(total, gbin_ref.shape[1:])
        f_ref[...] += dot(du_ref[...], win_ref[...].reshape(width, -1), NT)
        grad = dot(lowt_ref[...], du_ref[...]).astype(BF)
        grads_ref[0, :, 1] = grad.reshape(col_n, deep, -1)

    @pl.when(step == 2 * row_n - 1)
    def _():
        gain, bias, low, dog = 0.0, 0.0, 0.0, 0.0
        for cut in chunks(rows):
            d_hidden, normed = f_ref[cut, :], normed_ref[cut, :]
            d = norm_backward(d_hidden, normed, scale_ref[cut, 0:1], vec_ref[1:2, :])
            dres_ref[cut, :] = d
            d_low = d.astype(BF)
            df_ref[cut, :] = d_low
            gain = gain + column_sum(d_hidden * normed)
            bias = bias + column_sum(d_hidden)
            low = low + column_sum(d_low.astype(F32))
        f_ref[...] = dot(df_ref[...], wo_ref[...], NT)
        for cut in chunks(rows):
            d_o = f_ref[cut, :].astype(BF)
            pick = pick_ref[cut, :]
            is_glob = jnp.sum(pick.astype(F32), axis=1, keepdims=True) > 0.5
            dog = dog + dot(pick, d_o, TN)
            do_ref[cut, :] = jnp.where(is_glob, 0.0, f_ref[cut, :]).astype(BF)
        dog_ref[...] = dog.astype(BF)
        sums_ref[0:1, :] = low
        sums_ref[1:2, :] = gain
        sums_ref[2:3, :] = bias
        gout_ref[...] = dot(o_ref[...], df_ref[...], TN).astype(BF)


def vector_rows(a, row, gbin_ref, sums_ref, totals, col_n, length):
    hid, width = gbin_ref.shape[2], sums_ref.shape[1]
    deep = width // col_n
    span = totals[0].shape[1]
    grad = gbin_ref[jnp.bitwise_xor(row, a), 0:1, :]
    lines = [jnp.concatenate([grad[:, k : k + deep]] * col_n, axis=1) for k in range(0, hid, deep)]
    lines += [sums_ref[i : i + 1, :] for i in range(6)]
    head = lax.broadcasted_iota(jnp.int32, (1, width), 1) < HDIM
    for total in totals:
        wide = jnp.concatenate([total, jnp.zeros((1, width - span), F32)], axis=1)
        if a:
            wide = pltpu.roll(wide, width - a * HDIM, 1)
        wide = jnp.where(head, wide, 0.0)
        line = wide
        for c in range(1, col_n):
            line = line + pltpu.roll(wide, c * deep, 1)
        lines.append(line)
    lines.append(jnp.zeros((length - len(lines), width), F32))
    return jnp.concatenate(lines, axis=0).astype(BF)


def glob_backward(q, do, k, v, lse, og, keep):
    count, wide = q.shape
    heads = range(0, wide, HDIM)
    lse = jnp.concatenate([lse[:, h : h + 1] for h in heads], axis=0)
    q, do = stacked(q, 0.125).astype(BF), stacked(do, 1.0)
    inner = jnp.sum(do * jnp.concatenate([og] * len(heads), axis=0), axis=1, keepdims=True)
    do = do.astype(BF)
    p = jnp.exp(dot(q, k, NT) + keep - lse)
    p = jnp.where(keep < 0.0, 0.0, p)
    ds = (p * (dot(do, v, NT) - inner)).astype(BF)
    dq = (unstacked(dot(ds, k), count) * 0.125).astype(BF)
    return dq, dot(ds, q, TN), dot(p.astype(BF), do, TN)


def entry_backward_kernel(at_ref, *refs, row_n, col_n, calls, shares, last, more):
    dqs, dks, dvs, refs = refs[:calls], refs[calls : 2 * calls], refs[2 * calls : 3 * calls], refs[3 * calls :]
    qg_ref, dog_ref, k_ref, v_ref, lse_ref, og_ref, keys_ref, refs = *refs[:7], refs[7:]
    xs, refs = refs[:4], refs[4:]
    pieces, refs = refs[: row_n * col_n], refs[row_n * col_n :]
    if last:
        before_ref, earlier_ref, gbin_ref, sums_ref, keep_ref, send_ref, dx_ref = refs
    else:
        gout_ref, keep_ref, send_ref, dx_ref, totals_ref = refs
    row, col = at_ref[0], at_ref[1]
    span = row_n * HDIM
    sizes = [x.shape[0] for x in xs]
    starts = [sum(sizes[:g]) for g in range(4)]
    own = slice(starts[1], starts[2])

    def out_rows(a):
        return send_ref if a & 1 else keep_ref

    totals = []
    for i in range(shares):
        lane = slice(i * span, (i + 1) * span)
        call = i * calls // shares
        here = slice(0, span) if calls == shares else lane
        dq_ref, dk_ref, dv_ref = dqs[call], dks[call], dvs[call]
        dqg, dkg, dvg = glob_backward(
            qg_ref[:, lane], dog_ref[:, lane], k_ref[own, lane], v_ref[own, lane],
            lse_ref[:, lane], og_ref[:, lane], keys_ref[...],
        )
        dk_own = (dk_ref[own, here].astype(F32) + dkg).astype(BF)
        dv_own = (dv_ref[own, here].astype(F32) + dvg).astype(BF)
        parts = []
        for g in range(4):
            rows = slice(starts[g], starts[g] + sizes[g])
            dk = dk_own if g == 1 else dk_ref[rows, here]
            dv = dv_own if g == 1 else dv_ref[rows, here]
            dq = dq_ref[:, here] if g == 1 else dqg if g == 3 else None
            parts.append((dq, dk, dv))
        for kind in range(3):
            grad, total = 0.0, 0.0
            for g in range(4):
                term = parts[g][kind]
                if term is not None:
                    grad = grad + dot(term, xs[g][...], TN)
                    if kind != 1:
                        total = total + column_sum(term.astype(F32))
            if kind != 1:
                totals.append(total)
            for a in range(row_n):
                at = (i * 3 + kind) * HDIM
                block = grad[a * HDIM : (a + 1) * HDIM, :].astype(BF)
                out_rows(a)[a // 2, at : at + HDIM, :] = block
        mats = []
        for b in range(col_n):
            refs_b = [pieces[a * col_n + b] for a in range(row_n)]
            mats.append([share_rows(refs_b, i, kind) for kind in range(3)])
        mats = [
            jnp.concatenate(in_order([mats[b][kind] for b in range(col_n)], col), axis=1)
            for kind in range(3)
        ]
        for g in range(4):
            rows = slice(starts[g], starts[g] + sizes[g])
            value = before_ref[rows, :] if last and i == 0 else 0.0
            for kind in range(3):
                if parts[g][kind] is not None:
                    value = value + dot(parts[g][kind], mats[kind])
            if i == 0:
                dx_ref[rows, :] = value
            else:
                dx_ref[rows, :] += value
    at = 3 * shares * HDIM
    if last:
        totals = [earlier_ref[i : i + 1, :] for i in range(more[1])] + totals
        for a in range(row_n):
            out_rows(a)[a // 2, at : at + more[0], :] = vector_rows(
                a, row, gbin_ref, sums_ref, totals, col_n, more[0]
            )
    else:
        totals.append(jnp.zeros((totals_ref.shape[0] - len(totals), span), F32))
        totals_ref[...] = jnp.concatenate(totals, axis=0)
        heads = gout_ref.shape[0] // span
        for a in range(row_n):
            for i in range(heads):
                here = (i * row_n + a) * HDIM
                out_rows(a)[a // 2, at + i * HDIM : at + (i + 1) * HDIM, :] = gout_ref[
                    here : here + HDIM, :
                ]


def both_heads(value, scale):
    return jnp.concatenate([one_head(value, half, scale) for half in (0, 1)], axis=0)


def apart(value):
    size = value.shape[0] // 2
    return jnp.where(lanes((size, value.shape[1])), value[:size], value[size:])


def attend_forward_kernel(q_ref, k_ref, v_ref, bw_ref, bg_ref, o_ref, lse_ref, *, block, glob_at):
    count, window = bw_ref.shape[0], bw_ref.shape[2]
    glob = bg_ref.shape[2]
    kg, vg = k_ref[glob_at : glob_at + glob, :], v_ref[glob_at : glob_at + glob, :]
    for i in range(count):
        rows = slice(i * block, (i + 1) * block)
        span = slice(i * block, i * block + window)
        k, v = k_ref[span, :], v_ref[span, :]
        qs = both_heads(q_ref[rows, :], 0.125)
        bw, bg = bw_ref[i], bg_ref[i]
        sw = dot(qs, k, NT) + jnp.concatenate([bw, bw], axis=0)
        sg = dot(qs, kg, NT) + jnp.concatenate([bg, bg], axis=0)
        m = jnp.maximum(jnp.max(sw, axis=1, keepdims=True), jnp.max(sg, axis=1, keepdims=True))
        pw, pg = jnp.exp(sw - m), jnp.exp(sg - m)
        total = jnp.sum(pw, axis=1, keepdims=True) + jnp.sum(pg, axis=1, keepdims=True)
        o = (dot(pw.astype(BF), v) + dot(pg.astype(BF), vg)) * (1.0 / total)
        o_ref[rows, :] = apart(o).astype(BF)
        lse_ref[rows, :] = apart(jnp.broadcast_to(m + jnp.log(total), o.shape))


def attend_backward_kernel(
    q_ref, do_ref, k_ref, v_ref, lse_ref, bw_ref, bg_ref,
    dq_ref, dk_ref, dv_ref, dk_acc, dv_acc, *, block, glob_at,
):
    count, window = bw_ref.shape[0], bw_ref.shape[2]
    glob = bg_ref.shape[2]
    dk_acc[...] = jnp.zeros_like(dk_acc)
    dv_acc[...] = jnp.zeros_like(dv_acc)
    at_glob = slice(glob_at, glob_at + glob)
    kg, vg = k_ref[at_glob, :], v_ref[at_glob, :]
    for i in range(count):
        rows = slice(i * block, (i + 1) * block)
        span = slice(i * block, i * block + window)
        k, v = k_ref[span, :], v_ref[span, :]
        qs, dos = both_heads(q_ref[rows, :], 0.125), both_heads(do_ref[rows, :], 1.0)
        lse = jnp.concatenate([lse_ref[rows, h : h + 1] for h in (0, HDIM)], axis=0)
        bw, bg = bw_ref[i], bg_ref[i]
        pw = jnp.exp(dot(qs, k, NT) + jnp.concatenate([bw, bw], axis=0) - lse)
        pg = jnp.exp(dot(qs, kg, NT) + jnp.concatenate([bg, bg], axis=0) - lse)
        tw, tg = dot(dos, v, NT), dot(dos, vg, NT)
        inner = jnp.sum(pw * tw, axis=1, keepdims=True) + jnp.sum(pg * tg, axis=1, keepdims=True)
        dsw, dsg = (pw * (tw - inner)).astype(BF), (pg * (tg - inner)).astype(BF)
        dq_ref[rows, :] = (apart(dot(dsw, k) + dot(dsg, kg)) * 0.125).astype(BF)
        turned_q, turned_do = qs.T, dos.T
        dk_acc[:, span] += dot(turned_q, dsw)
        dk_acc[:, at_glob] += dot(turned_q, dsg)
        dv_acc[:, span] += dot(turned_do, pw.astype(BF))
        dv_acc[:, at_glob] += dot(turned_do, pg.astype(BF))
    for acc, out in ((dk_acc, dk_ref), (dv_acc, dv_ref)):
        for at in range(0, glob_at, 128):
            out[at : at + 128, :] = acc[:, at : at + 128].T.astype(BF)
        out[at_glob, :] = acc[:, at_glob].T.astype(BF)


def by_pair(rows):
    return pl.BlockSpec((rows, PAIR), lambda h: (0, h))


def whole(value):
    return pl.BlockSpec(value.shape, lambda h: (0,) * value.ndim)


def params(mebibytes):
    return pltpu.CompilerParams(vmem_limit_bytes=mebibytes * 1024 * 1024)


SCALAR = pl.BlockSpec(memory_space=pltpu.SMEM)


def once(value):
    return pl.BlockSpec(value.shape, lambda *s: (0,) * value.ndim, pipeline_mode=pl.Buffered(1))


def fixed(shape):
    return pl.BlockSpec(shape, lambda *s: (0,) * len(shape))


def hbm(*values):
    return [pltpu.with_memory_space_constraint(v, pltpu.HBM) if v.ndim > 1 else v for v in values]


def to_hbm(shapes):
    return [pltpu.HBM(v.shape, v.dtype) for v in shapes]


def cost(flops, size):
    return pl.CostEstimate(flops=flops, bytes_accessed=size, transcendentals=0)


def project(at, vecs, xs, pieces, glob, row_n, col_n):
    rows, wide = xs[1].shape
    ext = sum(x.shape[0] for x in xs) + glob
    length, deep = pieces[0].shape
    span = row_n * HDIM
    local = wide // span
    more = glob * col_n
    lane = lambda n: pl.BlockSpec((n, span), lambda i: (0, i))
    shapes = [(rows, wide), (glob, wide), (ext, wide), (ext, wide)]
    outs = [jax.ShapeDtypeStruct(v, BF) for v in shapes]
    outs += [jax.ShapeDtypeStruct((3, glob, wide), F32), jax.ShapeDtypeStruct((glob, wide), BF)]
    last = pl.BlockSpec((more, deep), lambda i: (length // more - 1, 0), pipeline_mode=pl.Buffered(1))
    return pl.pallas_call(
        functools.partial(project_kernel, row_n=row_n, col_n=col_n),
        grid=(local,),
        in_specs=[SCALAR]
        + [once(v) for v in vecs]
        + [once(x) for x in xs]
        + [pl.BlockSpec((3 * HDIM, deep), lambda i: (i, 0)) for _ in pieces]
        + [last for _ in pieces],
        out_specs=[lane(n) for n, _ in shapes]
        + [pl.BlockSpec((3, glob, span), lambda i: (0, 0, i)), fixed((glob, wide))],
        out_shape=to_hbm(outs),
        compiler_params=params(24),
        cost_estimate=cost(6_000_000_000, 10_000_000),
        name="project",
    )(*hbm(at, *vecs, *xs, *pieces, *pieces))


def mlp(o_parts, vecs, col_vecs, at, state, other, step, pick, x, cot, weights, row_n, col_n):
    rows, width = x.shape
    deep, hid = width // col_n, weights.shape[2]
    glob = state.shape[1]
    here = lambda i: jnp.where(i < row_n, i, i - row_n)
    back = lambda i: jnp.maximum(i - row_n, 0)
    sds = jax.ShapeDtypeStruct
    outs = [
        sds((rows, width), F32), sds((row_n, col_n, 2, deep, hid), BF), sds((row_n, 8, hid), F32),
        sds((rows, width), F32), sds((rows, width), BF), sds((width, width), BF),
        sds((8, width), F32), sds((glob, width), BF), sds((glob, width), F32),
        sds((glob, width), F32),
    ]
    specs = [fixed(v.shape) for v in outs]
    specs[1] = pl.BlockSpec((1, col_n, 2, deep, hid), lambda i: (back(i), 0, 0, 0, 0))
    specs[2] = pl.BlockSpec((1, 8, hid), lambda i: (back(i), 0, 0))
    count = weights.shape[1] - 2 * deep
    raw = pl.BlockSpec(
        (row_n * col_n, count, hid), lambda i: (0, 2 * deep // count, 0), pipeline_mode=pl.Buffered(1)
    )
    small = [state, other, pick, x, cot]
    lists = [*o_parts, *vecs, *col_vecs]
    big = [(rows, width)] * 3
    return pl.pallas_call(
        functools.partial(
            mlp_kernel, row_n=row_n, col_n=col_n, calls=len(o_parts), bit=head_bit(step)
        ),
        grid=(2 * row_n,),
        in_specs=[once(v) for v in lists]
        + [SCALAR]
        + [once(v) for v in small]
        + [raw]
        + [pl.BlockSpec((col_n, deep, hid), lambda i, k=k: (here(i), k, 0)) for k in (0, 1)],
        out_specs=specs,
        out_shape=to_hbm(outs),
        scratch_shapes=[
            pltpu.VMEM((8, width), F32),
            pltpu.VMEM((row_n, 8, hid), F32),
            pltpu.VMEM((width, width), BF),
            pltpu.VMEM((rows, width), BF),
            pltpu.VMEM((rows, width), BF),
            pltpu.VMEM((width, rows), BF),
            pltpu.VMEM((row_n, rows, hid), BF),
            pltpu.VMEM((row_n, rows, hid), F32),
            *[pltpu.VMEM(v, F32) for v in big],
            pltpu.VMEM((rows, 128), F32),
            pltpu.VMEM((rows, width), BF),
            pltpu.VMEM((width, rows), BF),
            pltpu.VMEM((rows, hid), F32),
            pltpu.VMEM((rows, hid), BF),
        ],
        compiler_params=params(58),
        cost_estimate=cost(17_000_000_000, 40_000_000),
        name="mlp",
    )(*hbm(*lists, at, *small, weights, weights, weights))


def entry_backward(at, parts, globs, xs, pieces, row_n, col_n, first, shares, gout=None, last=None):
    width = xs[0].shape[1]
    span = row_n * HDIM
    local = width // span
    deep = width // col_n
    ext = sum(x.shape[0] for x in xs)
    lane = lambda v: pl.BlockSpec((v.shape[0], shares * span), lambda i: (0, first // shares))
    piece = pl.BlockSpec((3 * shares * HDIM, deep), lambda i: (first // shares, 0))
    qg, dog, k_ext, v_ext, lse, og, keep = globs
    args = [p[j] for j in range(3) for p in parts]
    specs = [SCALAR] + [once(v) for v in args]
    args += globs
    specs += [lane(v) for v in globs[:-1]] + [once(keep)]
    args += xs
    specs += [once(v) for v in xs]
    args += pieces
    specs += [piece for _ in pieces]
    rest = list(last) if last else [gout]
    args += rest
    specs += [once(v) for v in rest]
    length, more = 3 * shares * HDIM, None
    if last:
        lines = last[2].shape[2] // deep + 6 + 2 * local
        more = (-(-lines // 32) * 32, 2 * (local - shares))
        length += more[0]
    else:
        length += width // row_n
    shape = jax.ShapeDtypeStruct((row_n // 2, length, width), BF)
    outs = [shape, shape, jax.ShapeDtypeStruct((ext, width), F32)]
    if not last:
        outs.append(jax.ShapeDtypeStruct((8, span), F32))
    return pl.pallas_call(
        functools.partial(
            entry_backward_kernel, row_n=row_n, col_n=col_n, calls=len(parts), shares=shares,
            last=last is not None, more=more,
        ),
        grid=(1,),
        in_specs=specs,
        out_specs=[fixed(v.shape) for v in outs],
        out_shape=to_hbm(outs),
        compiler_params=params(48),
        cost_estimate=cost(3_000_000_000 * shares, 8_000_000 * shares),
        name="entry_backward",
    )(*hbm(at, *args))


def some_pairs(rows, first):
    return pl.BlockSpec((rows, PAIR), lambda h: (0, h + first))


def attend_forward(q, k_ext, v_ext, bias_w, bias_g, glob_at, first, count):
    rows = q.shape[0]
    ext = k_ext.shape[0]
    block = bias_w.shape[1]
    wide = count * PAIR
    return pl.pallas_call(
        functools.partial(attend_forward_kernel, block=block, glob_at=glob_at),
        grid=(count,),
        in_specs=[some_pairs(rows, first), some_pairs(ext, first), some_pairs(ext, first)]
        + [whole(bias_w), whole(bias_g)],
        out_specs=[by_pair(rows), by_pair(rows)],
        out_shape=to_hbm(
            [jax.ShapeDtypeStruct((rows, wide), BF), jax.ShapeDtypeStruct((rows, wide), F32)]
        ),
        compiler_params=params(20),
        cost_estimate=pl.CostEstimate(
            flops=3_500_000_000, bytes_accessed=4_000_000, transcendentals=1_700_000
        ),
        name="attend_forward",
    )(*hbm(q, k_ext, v_ext, bias_w, bias_g))


def attend_backward(q, do, k_ext, v_ext, lse, bias_w, bias_g, glob_at, first, count, inside):
    rows = q.shape[0]
    ext = k_ext.shape[0]
    block = bias_w.shape[1]
    wide = count * PAIR
    return pl.pallas_call(
        functools.partial(attend_backward_kernel, block=block, glob_at=glob_at),
        grid=(count,),
        in_specs=[some_pairs(rows, first), some_pairs(rows, first)]
        + [some_pairs(ext, first), some_pairs(ext, first), some_pairs(rows, inside)]
        + [whole(bias_w), whole(bias_g)],
        out_specs=[by_pair(rows), by_pair(ext), by_pair(ext)],
        out_shape=to_hbm(
            [
                jax.ShapeDtypeStruct((rows, wide), BF),
                jax.ShapeDtypeStruct((ext, wide), BF),
                jax.ShapeDtypeStruct((ext, wide), BF),
            ]
        ),
        scratch_shapes=[pltpu.VMEM((PAIR, ext), F32), pltpu.VMEM((PAIR, ext), F32)],
        compiler_params=params(24),
        cost_estimate=pl.CostEstimate(
            flops=8_000_000_000, bytes_accessed=5_000_000, transcendentals=1_700_000
        ),
        name="attend_backward",
    )(*hbm(q, do, k_ext, v_ext, lse, bias_w, bias_g))


def norm_forward(resid, gain, shift_by):
    center = jnp.mean(resid, axis=1, keepdims=True)
    apart = resid - center
    scale = lax.rsqrt(jnp.mean(apart * apart, axis=1, keepdims=True) + 1e-05)
    normed = apart * scale
    return normed * gain + shift_by, normed, scale


def norm_backward(grad, normed, scale, gain):
    scaled = grad * gain
    total = jnp.mean(scaled, axis=1, keepdims=True)
    mixed = jnp.mean(scaled * normed, axis=1, keepdims=True)
    return scale * (scaled - total - normed * mixed)


def on_device(
    hidden_in, w_query, b_query, w_key, w_value, b_value, w_out, b_out, gain_attn, bias_attn,
    w_in, b_in, w_ffout, b_ffout, gain_ffn, bias_ffn, glob_pos, cotangent,
):
    row_n, col_n = lax.axis_size("row"), lax.axis_size("col")
    row_i, col_i = lax.axis_index("row"), lax.axis_index("col")
    rows = hidden_in.shape[0]
    wide, deep = w_query.shape[1], w_query.shape[0]
    hid = w_in.shape[1]
    local = wide // HDIM
    glob_row = glob_pos[0]
    glob = glob_row.shape[0]
    me = row_i * col_n + col_i
    halo = Halo(rows, row_n * col_n)
    is_prompt = me < halo.half

    own_rows = me * rows + jnp.arange(rows, dtype=jnp.int32)
    flags = [row_i, col_i, is_prompt.astype(jnp.int32), me * rows]
    at = jnp.stack([jnp.asarray(v, jnp.int32) for v in flags])
    message = pack(at, glob_row[None], hidden_in, w_query.T, w_key.T, w_value.T, col_n)
    vectors = (b_query, b_value, b_in, b_out, gain_attn, bias_attn, b_ffout, gain_ffn, bias_ffn)
    message, x_sent, vectors, w_in, w_out, w_ffout = fence(
        message, hidden_in, vectors, w_in, w_out, w_ffout
    )
    b_query, b_value, b_in, b_out, gain_attn, bias_attn, b_ffout, gain_ffn, bias_ffn = vectors
    pieces = gather_far(message)
    x_left, x_right, hop = halo.fetch(x_sent, is_prompt)
    ratio = hid // deep
    both = jnp.concatenate(
        [w_in, w_ffout, jnp.concatenate(jnp.split(w_out, ratio, axis=0), axis=1)], axis=0
    ).astype(BF)
    vec_row = jnp.pad(b_query.reshape(local, HDIM), ((0, 16 - local), (0, 128 - HDIM)))
    vec_row += jnp.pad(b_value.reshape(local, HDIM), ((0, 16 - local), (HDIM, 128 - 2 * HDIM)))
    vec_row += jnp.pad(b_in.reshape(-1, 128), ((local, 16 - local - hid // 128), (0, 0)))
    vec_col = jnp.zeros((8, deep), F32)
    for i, v in enumerate((b_out, gain_attn, bias_attn, b_ffout, gain_ffn, bias_ffn)):
        vec_col += jnp.pad(v[None], ((i, 7 - i), (0, 0)))
    hop, vec_row, vec_col, both = fence(hop, vec_row, vec_col, both)
    weights = lax.all_gather(both, ("row", "col"), axis=0)
    row_vec, col_vec = {0: vec_row}, {0: vec_col}
    for bit in (1 << i for i in range((row_n - 1).bit_length())):
        row_vec.update({a ^ bit: swap(v, ("row", bit)) for a, v in list(row_vec.items())})
    for bit in (1 << i for i in range((col_n - 1).bit_length())):
        col_vec.update({b ^ bit: swap(v, ("col", bit)) for b, v in list(col_vec.items())})
    vecs = [row_vec[a] for a in range(row_n)]
    col_vecs = [col_vec[b] for b in range(col_n)]

    pieces = gather_near(pieces)
    names = [(a, b) for a in range(row_n) for b in range(col_n)]
    pick = (own_rows[:, None] == glob_row[None, :]).astype(BF)

    own_at, glob_at = WIN, 2 * WIN + rows
    block = min(rows, WIN)
    bias_w, bias_g = bias_blocks(own_rows, halo.key_rows(me, is_prompt), glob_row, block)
    keep = jnp.where(is_prompt, 0.0, NEG) * jnp.ones((1, rows), F32)
    piece_list = [pieces[k] for k in names]
    q, qg, k_ext, v_ext, state, x_glob = project(
        at, vecs, [x_left, hidden_in, x_right], piece_list, glob, row_n, col_n
    )
    xs = [x_left, hidden_in, x_right, x_glob]

    span = row_n * HDIM
    share = span // PAIR
    rounds = [step for step in far_steps() if step != ("row", row_n // 2)] + [NEAR]
    rounds = [rounds[:-1], rounds[-1:]]
    calls = [(0, (local - 1) * share), ((local - 1) * share, share)]
    o_parts, lse_parts = [], []
    for i, (first_pair, count) in enumerate(calls):
        o_part, lse_part = attend_forward(
            q, k_ext, v_ext, bias_w, bias_g, glob_at, first_pair, count
        )
        o_parts.append(o_part)
        lse_parts.append(lse_part)
        for step in rounds[i][: None if i == 0 else -1]:
            state = merge_states(state, swap(state, step), step)
        if i == 0:
            state, q, o_parts[-1] = fence(state, q, o_part)

    hidden_out, grads, grad_b_in, d_resid1, d_o, out_grads, sums, dog, og, lse_g = mlp(
        o_parts, vecs, col_vecs, at, state, swap(state, rounds[1][-1]), rounds[1][-1], pick,
        hidden_in, cotangent, weights, row_n, col_n,
    )
    grads = grads.reshape(row_n * col_n, 2 * deep, hid)
    grads = lax.psum_scatter(grads, ("row", "col"), scatter_dimension=0, tiled=True)[0]

    def attend_share(i, d_o):
        at_call = min(i // (local - 1), 1)
        inside = i * share - calls[at_call][0]
        return attend_backward(
            q, d_o, k_ext, v_ext, lse_parts[at_call], bias_w, bias_g, glob_at, i * share, share, inside
        )

    parts = []
    for i in range(local - 1):
        parts.append(attend_share(i, d_o))
        for step in rounds[i] if i < len(rounds) else []:
            dog = add_heads(dog, swap(dog, step), step)
        if i < local - 2:
            dog, d_o, parts[-1] = fence(dog, d_o, parts[-1])
    globs = [qg, dog, k_ext, v_ext, lse_g, og, keep]
    keep_rows, send_rows, dx, totals = entry_backward(
        at, parts, globs, xs, piece_list, row_n, col_n, 0, local - 1, gout=out_grads
    )
    near = near_pieces(at, keep_rows, swap(send_rows, NEAR), col_n)
    near, d_o = fence(near, d_o)
    part = attend_share(local - 1, d_o)
    keep_rows, send_rows, dx = entry_backward(
        at, [part], globs, xs, piece_list, row_n, col_n, local - 1, 1,
        last=(dx, totals, grad_b_in, sums),
    )
    own_first = seq_scatter(far_sum(near))
    got, grads, own_first = fence(swap(send_rows, NEAR), grads, own_first)
    grads = lax.psum(grads, "seq")
    near = near_pieces(at, keep_rows, got, col_n)
    near, dx = fence(near, dx)
    own_last = seq_scatter(far_sum(near))
    split = own_first.shape[0]
    both = seq_gather(jnp.concatenate([own_first, own_last], axis=0))
    entry_first = jnp.concatenate([v[:split] for v in both], axis=0).astype(F32)
    entry_last = jnp.concatenate([v[split:] for v in both], axis=0).astype(F32)
    _, grads = fence(entry_last, grads)
    grads = grads.astype(F32)

    dx_glob = group_sum(dx[glob_at:], lambda a, b, step: a + b)
    first, last = halo.give(dx[:WIN], dx[own_at + rows : glob_at], is_prompt)
    grad_x = d_resid1 + dx[own_at : own_at + rows]
    grad_x = grad_x + lax.dot_general(
        pick.astype(F32), dx_glob, NN, precision=lax.Precision.HIGHEST, preferred_element_type=F32
    )
    size = first.shape[0]
    grad_x = jnp.concatenate([grad_x[:size] + first, grad_x[size:]], axis=0)
    grad_x = jnp.concatenate([grad_x[:-size], grad_x[-size:] + last], axis=0)

    cut = 3 * (local - 1) * HDIM
    by_kind = jnp.concatenate([entry_first[:cut], entry_last[: 3 * HDIM]], axis=0)
    by_kind = by_kind.reshape(local, 3, HDIM, deep)
    grad_out = entry_first[cut:]
    tail = entry_last[3 * HDIM :]
    b_rows = hid // deep
    bias_rows = tail[b_rows + 6 : b_rows + 6 + 2 * local, :HDIM].reshape(local, 2, HDIM)
    col_vectors = tail[b_rows : b_rows + 6]
    return (
        hidden_out,
        grad_x,
        by_kind[:, 0].reshape(wide, deep).T,
        bias_rows[:, 0].reshape(wide),
        by_kind[:, 1].reshape(wide, deep).T,
        by_kind[:, 2].reshape(wide, deep).T,
        bias_rows[:, 1].reshape(wide),
        grad_out,
        col_vectors[0],
        col_vectors[1],
        col_vectors[2],
        grads[deep:],
        tail[:b_rows].reshape(-1),
        grads[:deep],
        col_vectors[3],
        col_vectors[4],
        col_vectors[5],
    )


def solution(mesh):
    tokens = P(("seq", "row", "col"), None)
    both, row, col = P("col", "row"), P("row"), P("col")
    in_specs = (
        tokens, both, row, both, both, row, P("row", "col"), col, col, col, both, row, both, col,
        col, col, P("seq", None), tokens,
    )
    out_specs = (
        tokens, tokens, both, row, both, both, row, P("row", "col"), col, col, col, both, row,
        both, col, col, col,
    )
    return jax.shard_map(
        on_device, mesh=mesh, in_specs=in_specs, out_specs=out_specs, check_vma=False
    )
```
